32 devices in a mesh: leaf: 2 (over core), row: 8 (over z, x), col: 2 (over y).
Axes of the slice: x: 2, y: 2, z: 4, core: 2. Of those that a mesh axis runs over, the one named last changes fastest.
Arguments:
- child_tiles: float32 [256, 64, 4096], P(('leaf', 'row'), None, 'col'), may hold values from -0.15625 to 0.15625
- block_mask: int32 [256, 64], P(('leaf', 'row'), 'col'), may hold values 0 or 1
- destination: int32 [256, 1], P(('leaf', 'row')), may hold values from 0 to 15; in each aligned block of 16 rows (0 to 15, 16 to 31, ...) at most 2 rows name the same one
Outputs:
- r_top: float32 [2, 128, 4096], P('leaf', None, 'col')
The draws below stay inside these ranges and needn't reach their ends.
Inputs may be any that keep to these rules, and one draw needn't show every extreme that they name: Among the tiles of one device, no destination is named more than 2 times, a bound that some block reaches.
All inputs are finite; a program needn't handle non-finite values. No bound on the sum of `block_mask` on one device may be relied on, other than what follows from the above.
Results may differ from the reference program's by a relative error of at most 0.0003.
Values sent between devices are 32-bit elements; how exact they have to be, the bound alone decides.
No kernel may reach another device: no remote copies, remote signals or barrier semaphores. Data moves between devices by JAX's collectives and lax.ppermute only.
A program may use at most 64 MiB of HBM per device.

```python
import math
import jax
import jax.numpy as jnp
import numpy as np
from jax import lax

BLOCK_EDGE = 64
PARENT_COLUMNS = 4096
CAP = 2
FRONTS = 2
NDEST = 16
TILES_DEV = 16
TILES = 256
NBLOCKS = 64
COLUMN_BLOCKS = 32
ELIMINATED_COLS = 128
N_LEAF = 2
N_ROW = 8
N_COL = 2


def place_ends(result, own_key, least, high):
    index_at = [jax.random.randint(jax.random.fold_in(own_key, axis), (), 0, length) for axis, length in enumerate(result.shape)]
    widest = result.shape.index(max(result.shape))
    next_to = index_at[:widest] + [(index_at[widest] + 1) % result.shape[widest]] + index_at[widest + 1:]
    return result.at[tuple(index_at)].set(least).at[tuple(next_to)].set(high)


def level_of(stream_key, extent, pieces, least, largest):
    factor_of = 1.0
    for position, shards_of in pieces:
        heights = jax.random.uniform(jax.random.fold_in(jax.random.fold_in(stream_key, 6), position), (shards_of,), jnp.float32, least / len(pieces), largest / len(pieces))
        factor_of = factor_of * jnp.repeat(jnp.exp(heights), extent[position] // shards_of).reshape((-1,) + (1,) * (len(extent) - 1 - position))
    return factor_of


def assign_block(stream_key, own, number, rows, number_of, top, reach, slope):
    order = jax.random.permutation(stream_key, number_of)
    crowded, usual = shares(number_of, rows * top, reach, slope, True), shares(number_of, rows * top, reach, slope, False)
    places = jnp.arange(number_of)

    def named(sizes, turn):
        used = int((sizes > 0).sum())
        fixed = max(1, used // 4)
        moved = fixed + (places - fixed + turn * (used - fixed)) % max(1, number_of - fixed)
        return jnp.zeros((number_of,), jnp.int32).at[order[jnp.where(places < fixed, places, moved)]].set(jnp.asarray(sizes, jnp.int32))

    sizes = jnp.where(number % 4 == 0, named(crowded, number // 4), named(usual, number - number // 4 - 1))
    mixed = jax.random.permutation(jax.random.fold_in(own, 3), number_of)
    donor, sink = mixed[0:number_of // 2 * 2:2], mixed[1:number_of // 2 * 2:2]
    room = jnp.minimum(sizes[donor] - 1, reach - sizes[sink]) // 2
    room = jnp.where((donor == order[0]) | (sink == order[0]) | (sizes[sink] == 0), 0, jnp.maximum(room, 0))
    moved = jax.random.randint(jax.random.fold_in(own, 4), (number_of // 2,), 0, 1 << 20) % (room + 1)
    sizes = sizes.at[donor].add(-moved).at[sink].add(moved)
    items = jnp.searchsorted(jnp.cumsum(sizes), jnp.arange(rows * top), side="right").astype(jnp.int32)
    table = items.reshape(top, rows).T
    table = table[jax.random.permutation(jax.random.fold_in(own, 1), rows)]
    turn = jax.random.randint(jax.random.fold_in(own, 2), (rows, 1), 0, top)
    return jnp.take_along_axis(table, (jnp.arange(top)[None, :] + turn) % top, axis=1)


def shares(number_of, total, bound, lean, full):
    loads = [(1 << 20) // math.isqrt(rank ** lean) + 1 for rank in range(1, number_of + 1)]
    largest = bound if full else min(bound, max(-(-total // number_of), total * loads[0] // sum(loads)))
    least = 1 if total - largest >= number_of - 1 else 0
    given, rest = [largest] + [least] * (number_of - 1), total - largest - least * (number_of - 1)
    while rest > 0:
        candidates = [i for i in range(1, number_of) if given[i] < largest] or [i for i in range(1, number_of) if given[i] < bound]
        mass, budget = sum([loads[i] for i in candidates]), rest
        for i in candidates:
            extra = min(bound - given[i], max(1, budget * loads[i] // mass), rest)
            given[i] = given[i] + extra
            rest = rest - extra
    return np.array(given)


def normal_values(key, dims, deviation, most, shards=(), kind=jnp.bfloat16):
    result = deviation * jax.random.normal(key, dims, jnp.float32)
    if shards:
        result = result * level_of(key, dims, shards, -0.22, 0.18)
    return jnp.clip(result, -most, most).astype(kind)


def setup_inputs(seed: int = 0) -> dict:
    arg_keys = jax.random.split(jax.random.key(seed), 4)
    child_tiles = normal_values(arg_keys[0], (TILES, BLOCK_EDGE, PARENT_COLUMNS), ((TILES_DEV * N_ROW * BLOCK_EDGE) ** -0.5), 0.15625, ((0, 16), (2, 2)), jnp.float32)
    block_mask = place_ends((jax.random.randint(arg_keys[1], (TILES, NBLOCKS), 0, 4) < 3).astype(jnp.int32), jax.random.fold_in(arg_keys[1], 1), 0, 1)
    destination_keys = jax.random.split(jax.random.fold_in(arg_keys[2], 1), TILES // TILES_DEV)
    destination_turns = jax.random.permutation(jax.random.fold_in(arg_keys[2], 3), TILES // TILES_DEV)
    destination = jax.vmap(lambda own, number: assign_block(jax.random.fold_in(arg_keys[2], 2), own, number, TILES_DEV, NDEST, 1, CAP, 1))(destination_keys, destination_turns).reshape((TILES, 1))
    return dict(child_tiles=child_tiles, block_mask=block_mask, destination=destination)


def front_top(child_tiles, block_mask, destination, front_id):
    per_front = NDEST // FRONTS
    owner_front = destination[:, 0] // per_front
    outside = (owner_front != front_id).astype(jnp.int32)
    picked_count = min(TILES, N_LEAF * N_ROW * per_front * CAP)
    order = jnp.argsort(outside, stable=True)[:picked_count].astype(jnp.int32)
    inside = (owner_front[order] == front_id).astype(jnp.float32)
    chosen = child_tiles[order].reshape(picked_count, BLOCK_EDGE, NBLOCKS, BLOCK_EDGE)
    masks = block_mask[order].astype(jnp.float32)
    chosen = chosen * masks[:, None, :, None] * inside[:, None, None, None]
    stacked_tiles = chosen.reshape(picked_count * BLOCK_EDGE, N_COL, COLUMN_BLOCKS, BLOCK_EDGE)
    stacked_tiles = stacked_tiles.transpose(0, 2, 1, 3).reshape(picked_count * BLOCK_EDGE, PARENT_COLUMNS)
    leading_rows = stacked_tiles[:, :ELIMINATED_COLS]
    orthogonal_factor, upper_leading = jnp.linalg.qr(leading_rows)
    diagonal_signs = jnp.sign(jnp.diagonal(upper_leading))
    upper_remainder = jnp.dot(orthogonal_factor.T, stacked_tiles[:, ELIMINATED_COLS:], precision=lax.Precision.HIGHEST)
    upper_eliminated = diagonal_signs[:, None] * jnp.concatenate([upper_leading, upper_remainder], axis=1)
    return upper_eliminated.reshape(ELIMINATED_COLS, COLUMN_BLOCKS, N_COL, BLOCK_EDGE).transpose(0, 2, 1, 3).reshape(ELIMINATED_COLS, PARENT_COLUMNS)

def reference(child_tiles, block_mask, destination):

    def one_front(front_id):
        return front_top(child_tiles, block_mask, destination, front_id)
    return lax.map(one_front, jnp.arange(FRONTS, dtype=jnp.int32))
```

```python
import functools
import math

import jax
import jax.numpy as jnp
from jax import lax
from jax.experimental import pallas as pl
from jax.experimental.pallas import tpu as pltpu
from jax.sharding import PartitionSpec as P

PANELS = 2
VMEM_LIMIT = 48 * 1024 * 1024
F32 = jnp.float32
BF16 = jnp.bfloat16
HIGHEST = lax.Precision.HIGHEST


def split(value):
    high = value.astype(BF16)
    return high, (value - high.astype(F32)).astype(BF16)


def dot_nt(a, b):
    return lax.dot_general(a, b, (((1,), (1,)), ((), ())), precision=HIGHEST, preferred_element_type=F32)


def prep_kernel(mask_ref, tiles_ref, lead_ref, wide_ref):
    tile_count, edge, _ = tiles_ref.shape
    blocks, columns = mask_ref.shape[1], wide_ref.shape[1]
    mask = mask_ref[...].astype(F32)
    rows = tiles_ref[...] * mask[:, :1].reshape(tile_count, 1, 1)
    flipped = rows.reshape(tile_count * edge, rows.shape[2]).T
    lead_ref[...] = flipped[:edge]
    spread = lax.broadcasted_iota(jnp.int32, (blocks, columns), 1) // edge
    spread = (spread == lax.broadcasted_iota(jnp.int32, (blocks, columns), 0)).astype(F32)
    wide_ref[...] = jnp.dot(mask, spread, preferred_element_type=F32)


def front_rows(dest_ref, lead, leaf, per_front, edge):
    place = lax.broadcasted_iota(jnp.int32, (1, lead.shape[1]), 1) // edge
    front = jnp.zeros_like(place)
    for tile in range(dest_ref.shape[0]):
        front = jnp.where(place == tile, dest_ref[tile, 0] // per_front, front)
    mine = front == leaf
    return jnp.where(mine, lead, 0.0), jnp.where(mine, 0.0, lead)


def panel_kernel(per_front, with_pair, info_ref, dest_ref, *refs):
    if with_pair:
        lead_ref, other_ref, tiles_ref, wide_ref, keep_ref, send_ref, lhs, gram_k, gram_s, high, low = refs
    else:
        lead_ref, tiles_ref, wide_ref, keep_ref, send_ref, lhs, gram_k, gram_s, high, low = refs
    tile_count, edge, width = tiles_ref.shape

    @pl.when(pl.program_id(0) == 0)
    def _():
        lead = lead_ref[...]
        kept, sent = front_rows(dest_ref, lead, info_ref[1], per_front, edge)
        for place, part in enumerate((kept, sent)):
            part_high, part_low = split(part)
            lhs[place * edge : (place + 1) * edge] = part_high
            lhs[(place + 2) * edge : (place + 3) * edge] = part_low
        if with_pair:
            other = other_ref[...]
            first = info_ref[2] == 0
            lead_0, lead_1 = jnp.where(first, other, lead), jnp.where(first, lead, other)
            parts = front_rows(dest_ref, lead_1, info_ref[1], per_front, edge)
            for part, own, gram in zip(parts, (kept, sent), (gram_k, gram_s)):
                pair = jnp.concatenate([dot_nt(part, lead_0), dot_nt(own, lead)], axis=1)
                place_slabs(pair, gram)
        else:
            for own, gram in zip((kept, sent), (gram_k, gram_s)):
                block = dot_nt(own, lead)
                place_slabs(jnp.concatenate([block[: edge // 2], block[edge // 2 :]], axis=1), gram)

    for tile in range(tile_count):
        value = tiles_ref[tile] * wide_ref[tile : tile + 1, :]
        value_high, value_low = split(value)
        high[tile * edge : (tile + 1) * edge] = value_high
        low[tile * edge : (tile + 1) * edge] = value_low
    big = jnp.dot(lhs[...], high[...], preferred_element_type=F32)
    small = jnp.dot(lhs[: 2 * edge], low[...], preferred_element_type=F32)
    total = big[: 2 * edge] + (big[2 * edge :] + small)
    keep_ref[0, :edge] = total[:edge]
    send_ref[0, :edge] = total[edge:]
    keep_ref[0, edge:] = gram_k[...]
    send_ref[0, edge:] = gram_s[...]


def place_slabs(value, out):
    across = out.shape[1] // value.shape[1]
    for slab in range(value.shape[0] // 8):
        down, right = slab // across, slab % across
        out[down * 8 : (down + 1) * 8, right * 128 : (right + 1) * 128] = value[slab * 8 : (slab + 1) * 8]


def take_slabs(value):
    across = value.shape[1] // 128
    pieces = []
    for slab in range(value.shape[0] // 8 * across):
        down, right = slab // across, slab % across
        pieces.append(value[down * 8 : (down + 1) * 8, right * 128 : (right + 1) * 128])
    return jnp.concatenate(pieces, axis=0)


def factor_kernel(info_ref, own_ref, pair_ref, out_ref):
    own, pair = take_slabs(own_ref[...]), take_slabs(pair_ref[...])
    edge = pair.shape[0]
    size = 2 * edge
    own = jnp.concatenate([own[:, :edge], own[:, edge:]], axis=0)
    cross, other = pair[:, :edge], pair[:, edge:]
    first = info_ref[2] == 0
    gram_00, gram_11 = jnp.where(first, own, other), jnp.where(first, other, own)
    lower = jnp.concatenate([cross, gram_11], axis=1)
    upper = jnp.concatenate([gram_00, cross.T], axis=1)
    whole = jnp.concatenate([upper, lower], axis=0)
    rows = [whole[8 * i : 8 * i + 8] for i in range(size // 8)]
    lane = lax.broadcasted_iota(jnp.int32, (1, size), 1)
    down = lax.broadcasted_iota(jnp.int32, (8, 1), 0)
    for k in range(size):
        group, inside = k // 8, k % 8
        pivot_row = rows[group][inside : inside + 1]
        pivot = pivot_row[:, k : k + 1]
        scale = 1.0 / pivot
        pivot_row = jnp.where(lane == k, pivot + 1.0, pivot_row)
        scaled = pivot_row * scale
        for g in range(group, size // 8):
            if g == group and inside == 7:
                continue
            column = rows[g][:, k : k + 1]
            if g == group:
                column = jnp.where(down > inside, column, 0.0)
            rows[g] = rows[g] - column * scaled
    for g in range(size // 8):
        row = down + 8 * g
        diagonal = jnp.sum(jnp.where(lane == row, rows[g], 0.0), axis=1, keepdims=True)
        unit = jnp.where(lane < row, rows[g], jnp.where(lane == row, 1.0, 0.0))
        out_ref[8 * g : 8 * g + 8] = unit * lax.rsqrt(diagonal)


def final_kernel(pieces, edge, info_ref, inverse_ref, *refs):
    own_refs, other_refs, out_ref = refs[:pieces], refs[pieces : 2 * pieces], refs[-1]
    width = own_refs[0].shape[1]
    inverse = inverse_ref[...]
    first = info_ref[2] == 0
    left, right = inverse[:, :edge], inverse[:, edge:]
    own_side, other_side = jnp.where(first, left, right), jnp.where(first, right, left)
    for near in range(pieces):
        product = jnp.dot(own_side, own_refs[near][:edge], precision=HIGHEST, preferred_element_type=F32)
        product += jnp.dot(other_side, other_refs[near][:edge], precision=HIGHEST, preferred_element_type=F32)
        place = jnp.bitwise_xor(info_ref[0], near)
        out_ref[0, :, pl.ds(pl.multiple_of(place * width, width), width)] = product
    lead = out_ref[0, :, :128]
    row = lax.broadcasted_iota(jnp.int32, lead.shape, 0)
    lane = lax.broadcasted_iota(jnp.int32, lead.shape, 1)
    column = lane + info_ref[3] * edge
    out_ref[0, :, :128] = jnp.where((lane < edge) & (column < row), 0.0, lead)


def vmem():
    return pl.BlockSpec(memory_space=pltpu.VMEM)


def smem():
    return pl.BlockSpec(memory_space=pltpu.SMEM)


def per_device(child_tiles, block_mask, destination):
    tile_count, edge, columns = child_tiles.shape
    rows = tile_count * edge
    row_count, col_count = lax.axis_size("row"), lax.axis_size("col")
    bits = row_count.bit_length() - 1
    split_bits = min(2, bits - 1, (columns // 128).bit_length() - 1)
    pieces = 1 << split_bits
    width = columns // pieces
    across = width // 128
    row, leaf, col = lax.axis_index("row"), lax.axis_index("leaf"), lax.axis_index("col")
    own_panel = col if col_count == PANELS else jnp.zeros_like(col)
    info = jnp.stack([row % pieces, leaf, own_panel, col]).astype(jnp.int32)
    params = pltpu.CompilerParams(vmem_limit_bytes=VMEM_LIMIT)

    lead, wide = pl.pallas_call(
        prep_kernel,
        out_shape=(jax.ShapeDtypeStruct((edge, rows), F32), jax.ShapeDtypeStruct((tile_count, columns), F32)),
        grid=(1,),
        in_specs=[
            pl.BlockSpec(block_mask.shape, lambda i: (0, 0)),
            pl.BlockSpec((tile_count, edge, 128), lambda i: (0, 0, 0)),
        ],
        out_specs=(pl.BlockSpec((edge, rows), lambda i: (0, 0)), pl.BlockSpec((tile_count, columns), lambda i: (0, 0))),
        compiler_params=params,
        name="lead_prep",
    )(block_mask, child_tiles)

    if col_count == PANELS:
        lead_own = lead
        lead_other = lax.ppermute(lead, "col", [(i, 1 - i) for i in range(PANELS)])
    else:
        gathered = lax.all_gather(lead, "col")
        lead_own, lead_other = gathered[0], gathered[1]

    def panel(lead_parts, with_pair):
        slabs = 4 * (1 + with_pair)
        extra = 8 * slabs // across
        shape = jax.ShapeDtypeStruct((pieces, edge + extra, width), F32)
        out = pl.BlockSpec((1, edge + extra, width), lambda i, info, dest: (i, 0, 0))
        whole = pl.BlockSpec((edge, rows), lambda i, info, dest: (0, 0))
        return pl.pallas_call(
            functools.partial(panel_kernel, row_count, with_pair),
            out_shape=(shape, shape),
            grid_spec=pltpu.PrefetchScalarGridSpec(
                num_scalar_prefetch=2,
                grid=(pieces,),
                in_specs=[whole] * len(lead_parts)
                + [
                    pl.BlockSpec((tile_count, edge, width), lambda i, info, dest: (0, 0, jnp.bitwise_xor(i, info[0]))),
                    pl.BlockSpec((tile_count, width), lambda i, info, dest: (0, jnp.bitwise_xor(i, info[0]))),
                ],
                out_specs=(out, out),
                scratch_shapes=[
                    pltpu.VMEM((4 * edge, rows), BF16),
                    pltpu.VMEM((extra, width), F32),
                    pltpu.VMEM((extra, width), F32),
                    pltpu.VMEM((rows, width), BF16),
                    pltpu.VMEM((rows, width), BF16),
                ],
            ),
            compiler_params=params,
            cost_estimate=pl.CostEstimate(
                flops=6 * 2 * edge * rows * columns, bytes_accessed=4 * rows * columns, transcendentals=0
            ),
            name="panel_pair" if with_pair else "panel_own",
        )(info, destination, *lead_parts, child_tiles, wide)

    def over_leaf(keep, send):
        return keep + lax.ppermute(send, "leaf", [(0, 1), (1, 0)])

    def over_row(value, bit):
        return lax.ppermute(value, "row", [(i, i ^ bit) for i in range(row_count)])

    def reduce_quarter(partial):
        total = partial[0]
        for near in range(1, pieces):
            total = total + over_row(partial[near], near)
        for bit in range(split_bits, bits):
            total = total + over_row(total, 1 << bit)
        return total

    def gather_quarters(total):
        return [total[:edge]] + [over_row(total[:edge], near) for near in range(1, pieces)]

    own_sum = reduce_quarter(over_leaf(*panel((lead_own,), False)))
    own_pieces = gather_quarters(own_sum)
    other_sum = reduce_quarter(over_leaf(*panel((lead_other, lead_own), True)))
    other_pieces = gather_quarters(other_sum)

    inverse = pl.pallas_call(
        factor_kernel,
        out_shape=jax.ShapeDtypeStruct((2 * edge, 2 * edge), F32),
        in_specs=[smem(), vmem(), vmem()],
        out_specs=vmem(),
        compiler_params=params,
        name="gram_factor",
    )(info, own_sum[edge:], other_sum[edge:])

    return pl.pallas_call(
        functools.partial(final_kernel, pieces, edge),
        out_shape=jax.ShapeDtypeStruct((1, 2 * edge, columns), F32),
        in_specs=[smem(), vmem()] + [vmem()] * (2 * pieces),
        out_specs=vmem(),
        compiler_params=params,
        name="apply_inverse",
    )(info, inverse, *own_pieces, *other_pieces)


def solution(mesh):
    in_specs = (
        P(("leaf", "row"), None, "col"),
        P(("leaf", "row"), "col"),
        P(("leaf", "row"), None),
    )
    out_specs = P("leaf", None, "col")
    return jax.shard_map(per_device, mesh=mesh, in_specs=in_specs, out_specs=out_specs, check_vma=False)
```

```python
import functools

import jax
import jax.numpy as jnp
from jax import lax
from jax.experimental import pallas as pl
from jax.experimental.pallas import tpu as pltpu
from jax.sharding import PartitionSpec as P

PANELS = 2
VMEM_LIMIT = 16 * 1024 * 1024
OWN_VMEM_LIMIT = 44 * 1024 * 1024
F32 = jnp.float32
BF16 = jnp.bfloat16
HIGHEST = lax.Precision.HIGHEST


def split(value):
    high = value.astype(BF16)
    return high, (value - high.astype(F32)).astype(BF16)


def dot_nt(a, b):
    return lax.dot_general(a, b, (((1,), (1,)), ((), ())), precision=HIGHEST, preferred_element_type=F32)


def prep_kernel(lead_ref, flipped_ref, mask_ref):
    edge = flipped_ref.shape[0]
    mask = lead_ref[:, edge:]
    flipped_ref[...] = (lead_ref[:, :edge] * mask[:, :, :1]).reshape(-1, edge).T
    mask_ref[...] = mask.reshape(mask_ref.shape)


def spread_mask(mask, columns, edge):
    blocks = mask.shape[1]
    over = lax.broadcasted_iota(jnp.int32, (blocks, columns), 1) // edge
    over = (over == lax.broadcasted_iota(jnp.int32, (blocks, columns), 0)).astype(F32)
    return jnp.dot(mask, over, preferred_element_type=F32)


def spread_front(dest_ref, leaf, per_front, rows):
    tile_count = dest_ref.shape[1]
    place = lax.broadcasted_iota(jnp.int32, (1, rows), 1) // (rows // tile_count)
    mine = jnp.zeros((1, rows), F32)
    for tile in range(tile_count):
        here = (dest_ref[0, tile] // per_front == leaf).astype(F32)
        mine = jnp.where(place == tile, here, mine)
    return mine


def by_front(lead, mine):
    return lead * mine, lead * (1.0 - mine)


def fill_factor(lhs, kept, sent, edge):
    for place, part in enumerate((kept, sent)):
        part_high, part_low = split(part)
        lhs[place * edge : (place + 1) * edge] = part_high
        lhs[(place + 2) * edge : (place + 3) * edge] = part_low


def panel_product(lhs, high, low, edge):
    big = jnp.dot(lhs, high, preferred_element_type=F32)
    small = jnp.dot(lhs[: 2 * edge], low, preferred_element_type=F32)
    return big[: 2 * edge] + (big[2 * edge :] + small)


def put_gram(blocks, out, edge):
    for near in range(out.shape[0]):
        place_slabs(blocks, out.at[near, edge:])


def halves_beside(block):
    return jnp.concatenate([block[: block.shape[0] // 2], block[block.shape[0] // 2 :]], axis=1)


def own_kernel(per_front, info_ref, dest_ref, mask_ref, lead_ref, tiles_ref, keep_ref, send_ref, high, low, mine_ref, lhs, held, wide_ref, total_ref, sems):
    tile_count, edge, columns = held.shape
    pieces, _, width = keep_ref.shape
    copies = [pltpu.make_async_copy(tiles_ref.at[tile], held.at[tile], sems.at[tile]) for tile in range(tile_count)]
    for copy in copies:
        copy.start()
    wide_ref[...] = spread_mask(mask_ref[...], columns, edge)
    mine_ref[...] = spread_front(dest_ref, info_ref[1], per_front, lead_ref.shape[1])
    lead = lead_ref[...]
    parts = by_front(lead, mine_ref[...])
    fill_factor(lhs, *parts, edge)
    gram = dot_nt(jnp.concatenate(parts, axis=0), lead)
    put_gram(halves_beside(gram[:edge]), keep_ref, edge)
    put_gram(halves_beside(gram[edge:]), send_ref, edge)
    group = max(1, 256 // edge)
    for first in range(0, tile_count, group):
        for tile in range(first, first + group):
            copies[tile].wait()
            value = held[tile] * wide_ref[tile : tile + 1, :]
            value_high, value_low = split(value)
            high[tile * edge : (tile + 1) * edge] = value_high
            low[tile * edge : (tile + 1) * edge] = value_low
        deep = slice(first * edge, (first + group) * edge)
        for piece in range(pieces):
            here = slice(piece * width, (piece + 1) * width)
            part = panel_product(lhs[:, deep], high[deep, here], low[deep, here], edge)
            if first + group < tile_count:
                total_ref[:, here] = part if first == 0 else total_ref[:, here] + part
                continue
            total = total_ref[:, here] + part if first else part
            near = jnp.bitwise_xor(info_ref[0], piece)
            keep_ref[near, :edge] = total[:edge]
            send_ref[near, :edge] = total[edge:]


def pair_kernel(with_other, info_ref, mine_ref, lead_ref, own_ref, high, low, keep_ref, send_ref, lhs):
    edge = lead_ref.shape[0]
    pieces, _, width = keep_ref.shape
    lead, own = lead_ref[...], own_ref[...]
    parts = by_front(lead, mine_ref[...])
    fill_factor(lhs, *parts, edge)
    both = jnp.concatenate(parts, axis=0)
    cross = dot_nt(both, own)
    other = dot_nt(both, lead) if with_other else None
    for place, out in enumerate((keep_ref, send_ref)):
        here = slice(place * edge, (place + 1) * edge)
        blocks = halves_beside(cross[here])
        if with_other:
            blocks = jnp.concatenate([blocks, halves_beside(other[here])], axis=0)
        put_gram(blocks, out, edge)
    for piece in range(pieces):
        here = slice(piece * width, (piece + 1) * width)
        total = panel_product(lhs[...], high[:, here], low[:, here], edge)
        near = jnp.bitwise_xor(info_ref[0], piece)
        keep_ref[near, :edge] = total[:edge]
        send_ref[near, :edge] = total[edge:]


def place_slabs(value, out):
    across = out.shape[1] // value.shape[1]
    for slab in range(value.shape[0] // 8):
        down, right = slab // across, slab % across
        out[down * 8 : (down + 1) * 8, right * 128 : (right + 1) * 128] = value[slab * 8 : (slab + 1) * 8]


def take_block(ref, edge, start=0):
    across = ref.shape[1] // 128
    slabs = []
    for slab in range(start, start + edge // 16):
        down, right = slab // across, slab % across
        slabs.append(ref[down * 8 : (down + 1) * 8, right * 128 : (right + 1) * 128])
    value = jnp.concatenate(slabs, axis=0)
    return jnp.concatenate([value[:, :edge], value[:, edge:]], axis=0)


STEP = 8


def inverse_factor(whole, put):
    size = whole.shape[0]
    groups = size // 8
    rows = [whole[8 * i : 8 * i + 8] for i in range(groups)]
    lane = lax.broadcasted_iota(jnp.int32, (8, size), 1)
    down = lax.broadcasted_iota(jnp.int32, (8, size), 0)
    span = range(STEP)
    for k in range(0, size, STEP):
        group, inside = k // 8, k % 8
        pivot = [jnp.broadcast_to(rows[group][inside + j : inside + j + 1], (8, size)) for j in span]
        entry = [[jnp.broadcast_to(pivot[i][:, k + j : k + j + 1], (8, size)) for j in range(i + 1)] for i in span]
        ratio = [[None] * STEP for _ in span]
        inverse = [None] * STEP
        for j in span:
            inverse[j] = 1.0 / entry[j][j]
            for i in range(j + 1, STEP):
                ratio[i][j] = entry[i][j] * inverse[j]
            for i in range(j + 1, STEP):
                for m in range(j + 1, i + 1):
                    entry[i][m] = entry[i][m] - ratio[i][j] * entry[m][j]
        solved = []
        for j in span:
            unit = jnp.where(lane < k, pivot[j], jnp.where(lane == k + j, 1.0, 0.0))
            for i in range(j):
                unit = unit - ratio[j][i] * solved[i]
            solved.append(unit)
            put(k + j, (unit * lax.rsqrt(entry[j][j]))[:1])
        if k + STEP == size:
            break
        front = [jnp.where(lane == k + j, pivot[j] + 1.0, pivot[j]) for j in span]
        for j in span:
            for i in range(j):
                front[j] = front[j] - ratio[j][i] * front[i]
        back = [front[j] * inverse[j] for j in span]
        for j in reversed(span):
            for i in range(j + 1, STEP):
                back[j] = back[j] - ratio[i][j] * back[i]
        for g in range((k + STEP) // 8, groups):
            change = None
            for j in span:
                term = jnp.broadcast_to(rows[g][:, k + j : k + j + 1], (8, size)) * back[j]
                change = term if change is None else change + term
            if g == group:
                change = jnp.where(down < inside + STEP, 0.0, change)
            rows[g] = rows[g] - change


def both_grams(info_ref, own_ref, other_ref, other_start, edge):
    own, other = take_block(own_ref, edge), take_block(other_ref, edge, other_start)
    first = info_ref[2] == 0
    return jnp.where(first, own, other), jnp.where(first, other, own)


def first_factor_kernel(start, info_ref, own_ref, other_ref, out_ref):
    edge = out_ref.shape[0]
    gram, _ = both_grams(info_ref, own_ref, other_ref, start, edge)

    def put(index, row):
        out_ref[index : index + 1] = row

    inverse_factor(gram, put)


def rest_factor_kernel(start, info_ref, own_ref, other_ref, pair_ref, corner_ref, out_ref):
    edge = corner_ref.shape[0]
    _, gram = both_grams(info_ref, own_ref, other_ref, start, edge)
    cross = take_block(pair_ref, edge)
    cross = jnp.where(info_ref[2] == 0, cross, cross.T)
    corner = corner_ref[...]
    lower = dot_nt(cross, corner)
    both = jnp.dot(lower, corner, precision=HIGHEST, preferred_element_type=F32)
    out_ref[:edge, :edge] = corner
    out_ref[:edge, edge:] = jnp.zeros_like(corner)

    def put(index, row):
        out_ref[edge + index : edge + index + 1, edge:] = row

    inverse_factor(gram - dot_nt(lower, lower), put)
    out_ref[edge:, :edge] = -jnp.dot(out_ref[edge:, edge:], both, precision=HIGHEST, preferred_element_type=F32)


def final_kernel(pieces, edge, info_ref, inverse_ref, *refs):
    own_refs, other_refs, (out_ref, held, sems) = refs[:pieces], refs[pieces : 2 * pieces], refs[2 * pieces :]
    width = own_refs[0].shape[1]
    inverse = inverse_ref[...]
    first = info_ref[2] == 0
    left, right = inverse[:, :edge], inverse[:, edge:]
    inverse = jnp.concatenate([jnp.where(first, left, right), jnp.where(first, right, left)], axis=1)
    inverse_high, inverse_low = split(inverse)
    both = jnp.concatenate([inverse_high, inverse_low], axis=0)
    row = lax.broadcasted_iota(jnp.int32, (2 * edge, width), 0)
    lane = lax.broadcasted_iota(jnp.int32, (2 * edge, width), 1)
    copies = []
    for near in range(pieces):
        part = jnp.concatenate([own_refs[near][:edge], other_refs[near][:edge]], axis=0)
        part_high, part_low = split(part)
        product = jnp.dot(both, part_high, preferred_element_type=F32)
        small = jnp.dot(inverse_high, part_low, preferred_element_type=F32)
        product = product[: 2 * edge] + (product[2 * edge :] + small)
        place = jnp.bitwise_xor(info_ref[0], near)
        place_lane = lane + place * width
        early = (place_lane < edge) & (place_lane + info_ref[3] * edge < row)
        held[near] = jnp.where(early, 0.0, product)
        copy = pltpu.make_async_copy(
            held.at[near],
            out_ref.at[0, :, pl.ds(pl.multiple_of(place * width, width), width)],
            sems.at[near],
        )
        copy.start()
        copies.append(copy)
    for copy in copies:
        copy.wait()


def vmem():
    return pl.BlockSpec(memory_space=pltpu.VMEM)


def smem():
    return pl.BlockSpec(memory_space=pltpu.SMEM)


def per_device(child_tiles, block_mask, destination):
    tile_count, edge, columns = child_tiles.shape
    rows = tile_count * edge
    row_count, col_count = lax.axis_size("row"), lax.axis_size("col")
    bits = row_count.bit_length() - 1
    split_bits = min(2, bits - 1, (columns // 128).bit_length() - 1)
    pieces = 1 << split_bits
    width = columns // pieces
    row, leaf, col = lax.axis_index("row"), lax.axis_index("leaf"), lax.axis_index("col")
    own_panel = col if col_count == PANELS else jnp.zeros_like(col)
    info = jnp.stack([row % pieces, leaf, own_panel, col]).astype(jnp.int32)
    params = pltpu.CompilerParams(vmem_limit_bytes=VMEM_LIMIT)
    wide_params = pltpu.CompilerParams(vmem_limit_bytes=OWN_VMEM_LIMIT)

    blocks = columns // edge
    mask_row = jnp.pad(block_mask.astype(F32), ((0, 0), (0, edge - blocks)))[:, None]
    lead, mask = pl.pallas_call(
        prep_kernel,
        out_shape=(jax.ShapeDtypeStruct((edge, rows), F32), jax.ShapeDtypeStruct((tile_count, edge), F32)),
        in_specs=[vmem()],
        out_specs=(vmem(), vmem()),
        compiler_params=params,
        name="lead_prep",
    )(jnp.concatenate([child_tiles[:, :, :edge], mask_row], axis=1))

    if col_count == PANELS:
        lead_own = lead
        lead_other = lax.ppermute(lead, "col", [(i, 1 - i) for i in range(PANELS)])
    else:
        gathered = lax.all_gather(lead, "col")
        lead_own, lead_other = gathered[0], gathered[1]

    swap = col_count == PANELS
    gram_rows = edge * edge // width
    factor = pltpu.VMEM((4 * edge, rows), BF16)
    work = pl.CostEstimate(flops=12 * edge * rows * columns, bytes_accessed=4 * rows * columns, transcendentals=0)

    def sums(extra):
        return jax.ShapeDtypeStruct((pieces, edge + extra, width), F32)

    halves = jax.ShapeDtypeStruct((rows, columns), BF16)
    keep, send, high, low, mine = pl.pallas_call(
        functools.partial(own_kernel, row_count),
        out_shape=(sums(gram_rows), sums(gram_rows), halves, halves, jax.ShapeDtypeStruct((1, rows), F32)),
        in_specs=[smem(), smem(), vmem(), vmem(), pl.BlockSpec(memory_space=pl.ANY)],
        out_specs=(vmem(),) * 5,
        scratch_shapes=[
            factor,
            pltpu.VMEM((tile_count, edge, columns), F32),
            pltpu.VMEM((tile_count, columns), F32),
            pltpu.VMEM((2 * edge, columns), F32),
            pltpu.SemaphoreType.DMA((tile_count,)),
        ],
        compiler_params=wide_params,
        cost_estimate=work,
        name="panel_own",
    )(info, destination.reshape(1, tile_count), mask, lead_own, child_tiles)

    def over_leaf(keep, send):
        return keep + lax.ppermute(send, "leaf", [(0, 1), (1, 0)])

    def over_row(value, bit):
        return lax.ppermute(value, "row", [(i, i ^ bit) for i in range(row_count)])

    def reduce_near(partial):
        total = partial[0]
        for near in range(1, pieces):
            total = total + over_row(partial[near], near)
        return total

    def reduce_far(total):
        for bit in range(split_bits, bits):
            total = total + over_row(total, 1 << bit)
        return total

    def gather_pieces(total):
        return [total[:edge]] + [over_row(total[:edge], near) for near in range(1, pieces)]

    send, lead_other = lax.optimization_barrier((send, lead_other))
    own_sum = reduce_far(reduce_near(over_leaf(keep, send)))
    own_pieces = gather_pieces(own_sum)

    pair_rows = gram_rows if swap else 2 * gram_rows
    keep, send = pl.pallas_call(
        functools.partial(pair_kernel, not swap),
        out_shape=(sums(pair_rows), sums(pair_rows)),
        in_specs=[smem(), vmem(), vmem(), vmem(), vmem(), vmem()],
        out_specs=(vmem(),) * 2,
        scratch_shapes=[factor],
        compiler_params=params,
        cost_estimate=work,
        name="panel_pair",
    )(info, mine, lead_other, lead_own, high, low)
    other_sum = reduce_far(reduce_near(over_leaf(keep, send)))

    own_gram = own_sum[edge:]
    if swap:
        other_gram, start = lax.ppermute(own_gram, "col", [(i, 1 - i) for i in range(PANELS)]), 0
    else:
        other_gram, start = other_sum[edge:], edge // 16
    corner = pl.pallas_call(
        functools.partial(first_factor_kernel, start),
        out_shape=jax.ShapeDtypeStruct((edge, edge), F32),
        in_specs=[smem(), vmem(), vmem()],
        out_specs=vmem(),
        compiler_params=params,
        cost_estimate=pl.CostEstimate(flops=work.flops // 2, bytes_accessed=work.bytes_accessed // 2, transcendentals=0),
        name="gram_factor_first",
    )(info, own_gram, other_gram)
    if swap:
        other_sum, corner = lax.optimization_barrier((other_sum, corner))
    other_pieces = gather_pieces(other_sum)
    pair_gram = other_sum[edge:]
    inverse = pl.pallas_call(
        functools.partial(rest_factor_kernel, start),
        out_shape=jax.ShapeDtypeStruct((2 * edge, 2 * edge), F32),
        in_specs=[smem()] + [vmem()] * 4,
        out_specs=vmem(),
        compiler_params=params,
        name="gram_factor_rest",
    )(info, own_gram, other_gram, pair_gram, corner)

    return pl.pallas_call(
        functools.partial(final_kernel, pieces, edge),
        out_shape=jax.ShapeDtypeStruct((1, 2 * edge, columns), F32),
        in_specs=[smem(), vmem()] + [vmem()] * (2 * pieces),
        out_specs=pl.BlockSpec(memory_space=pl.ANY),
        scratch_shapes=[pltpu.VMEM((pieces, 2 * edge, width), F32), pltpu.SemaphoreType.DMA((pieces,))],
        compiler_params=params,
        name="apply_inverse",
    )(info, inverse, *own_pieces, *other_pieces)


def solution(mesh):
    in_specs = (
        P(("leaf", "row"), None, "col"),
        P(("leaf", "row"), "col"),
        P(("leaf", "row"), None),
    )
    out_specs = P("leaf", None, "col")
    return jax.shard_map(per_device, mesh=mesh, in_specs=in_specs, out_specs=out_specs, check_vma=False)
```

```python
import functools

import jax
import jax.numpy as jnp
from jax import lax
from jax.experimental import pallas as pl
from jax.experimental.pallas import tpu as pltpu
from jax.sharding import PartitionSpec as P

PANELS = 2
VMEM_LIMIT = 16 * 1024 * 1024
OWN_VMEM_LIMIT = 44 * 1024 * 1024
F32 = jnp.float32
BF16 = jnp.bfloat16
HIGHEST = lax.Precision.HIGHEST


def split(value):
    high = value.astype(BF16)
    return high, (value - high.astype(F32)).astype(BF16)


def dot_nt(a, b):
    return lax.dot_general(a, b, (((1,), (1,)), ((), ())), precision=HIGHEST, preferred_element_type=F32)


def prep_kernel(lead_ref, flipped_ref, mask_ref):
    edge = flipped_ref.shape[0]
    tile_count, blocks = mask_ref.shape
    mask = lead_ref[tile_count, :tile_count, :blocks]
    mask_ref[...] = mask
    flipped_ref[...] = (lead_ref[:tile_count] * mask[:, :1].reshape(tile_count, 1, 1)).reshape(-1, edge).T


def spread_mask(mask, columns, edge):
    blocks = mask.shape[1]
    over = lax.broadcasted_iota(jnp.int32, (blocks, columns), 1) // edge
    over = (over == lax.broadcasted_iota(jnp.int32, (blocks, columns), 0)).astype(F32)
    return jnp.dot(mask, over, preferred_element_type=F32)


def spread_front(dest_ref, leaf, per_front, rows):
    tile_count = dest_ref.shape[1]
    place = lax.broadcasted_iota(jnp.int32, (1, rows), 1) // (rows // tile_count)
    mine = jnp.zeros((1, rows), F32)
    for tile in range(tile_count):
        here = (dest_ref[0, tile] // per_front == leaf).astype(F32)
        mine = jnp.where(place == tile, here, mine)
    return mine


def by_front(lead, mine):
    return lead * mine, lead * (1.0 - mine)


def fill_factor(lhs, kept, sent, edge):
    for place, part in enumerate((kept, sent)):
        part_high, part_low = split(part)
        lhs[place * edge : (place + 1) * edge] = part_high
        lhs[(place + 2) * edge : (place + 3) * edge] = part_low


def panel_product(lhs, high, low, edge):
    big = jnp.dot(lhs, high, preferred_element_type=F32)
    small = jnp.dot(lhs[: 2 * edge], low, preferred_element_type=F32)
    return big[: 2 * edge] + (big[2 * edge :] + small)


def put_gram(blocks, out, edge):
    for near in range(out.shape[0]):
        place_slabs(blocks, out.at[near, edge:])


def halves_beside(block):
    return jnp.concatenate([block[: block.shape[0] // 2], block[block.shape[0] // 2 :]], axis=1)


def own_kernel(per_front, info_ref, dest_ref, mask_ref, lead_ref, tiles_ref, keep_ref, send_ref, high, low, mine_ref, lhs, held, wide_ref, total_ref, sems):
    tile_count, edge, columns = held.shape
    pieces, _, width = keep_ref.shape
    copies = [pltpu.make_async_copy(tiles_ref.at[tile], held.at[tile], sems.at[tile]) for tile in range(tile_count)]
    for copy in copies:
        copy.start()
    wide_ref[...] = spread_mask(mask_ref[...], columns, edge)
    mine_ref[...] = spread_front(dest_ref, info_ref[1], per_front, lead_ref.shape[1])
    lead = lead_ref[...]
    parts = by_front(lead, mine_ref[...])
    fill_factor(lhs, *parts, edge)
    gram = dot_nt(jnp.concatenate(parts, axis=0), lead)
    put_gram(halves_beside(gram[:edge]), keep_ref, edge)
    put_gram(halves_beside(gram[edge:]), send_ref, edge)
    group = max(1, 256 // edge)
    for first in range(0, tile_count, group):
        for tile in range(first, first + group):
            copies[tile].wait()
            value = held[tile] * wide_ref[tile : tile + 1, :]
            value_high, value_low = split(value)
            high[tile * edge : (tile + 1) * edge] = value_high
            low[tile * edge : (tile + 1) * edge] = value_low
        deep = slice(first * edge, (first + group) * edge)
        for piece in range(pieces):
            here = slice(piece * width, (piece + 1) * width)
            part = panel_product(lhs[:, deep], high[deep, here], low[deep, here], edge)
            if first + group < tile_count:
                total_ref[:, here] = part if first == 0 else total_ref[:, here] + part
                continue
            total = total_ref[:, here] + part if first else part
            near = jnp.bitwise_xor(info_ref[0], piece)
            keep_ref[near, :edge] = total[:edge]
            send_ref[near, :edge] = total[edge:]


def pair_kernel(with_other, info_ref, mine_ref, lead_ref, own_ref, high, low, keep_ref, send_ref, lhs):
    edge = lead_ref.shape[0]
    pieces, _, width = keep_ref.shape
    lead, own = lead_ref[...], own_ref[...]
    parts = by_front(lead, mine_ref[...])
    fill_factor(lhs, *parts, edge)
    both = jnp.concatenate(parts, axis=0)
    cross = dot_nt(both, own)
    other = dot_nt(both, lead) if with_other else None
    for place, out in enumerate((keep_ref, send_ref)):
        here = slice(place * edge, (place + 1) * edge)
        blocks = halves_beside(cross[here])
        if with_other:
            blocks = jnp.concatenate([blocks, halves_beside(other[here])], axis=0)
        put_gram(blocks, out, edge)
    for piece in range(pieces):
        here = slice(piece * width, (piece + 1) * width)
        total = panel_product(lhs[...], high[:, here], low[:, here], edge)
        near = jnp.bitwise_xor(info_ref[0], piece)
        keep_ref[near, :edge] = total[:edge]
        send_ref[near, :edge] = total[edge:]


def place_slabs(value, out):
    across = out.shape[1] // value.shape[1]
    for slab in range(value.shape[0] // 8):
        down, right = slab // across, slab % across
        out[down * 8 : (down + 1) * 8, right * 128 : (right + 1) * 128] = value[slab * 8 : (slab + 1) * 8]


def take_block(ref, edge, start=0):
    across = ref.shape[1] // 128
    slabs = []
    for slab in range(start, start + edge // 16):
        down, right = slab // across, slab % across
        slabs.append(ref[down * 8 : (down + 1) * 8, right * 128 : (right + 1) * 128])
    value = jnp.concatenate(slabs, axis=0)
    return jnp.concatenate([value[:, :edge], value[:, edge:]], axis=0)


STEP = 8


def inverse_factor(whole, put):
    size = whole.shape[0]
    groups = size // 8
    rows = [whole[8 * i : 8 * i + 8] for i in range(groups)]
    lane = lax.broadcasted_iota(jnp.int32, (8, size), 1)
    down = lax.broadcasted_iota(jnp.int32, (8, size), 0)
    span = range(STEP)
    for k in range(0, size, STEP):
        group, inside = k // 8, k % 8
        pivot = [jnp.broadcast_to(rows[group][inside + j : inside + j + 1], (8, size)) for j in span]
        entry = [[jnp.broadcast_to(pivot[i][:, k + j : k + j + 1], (8, size)) for j in range(i + 1)] for i in span]
        ratio = [[None] * STEP for _ in span]
        inverse = [None] * STEP
        for j in span:
            inverse[j] = 1.0 / entry[j][j]
            for i in range(j + 1, STEP):
                ratio[i][j] = entry[i][j] * inverse[j]
            for i in range(j + 1, STEP):
                for m in range(j + 1, i + 1):
                    entry[i][m] = entry[i][m] - ratio[i][j] * entry[m][j]
        solved = []
        for j in span:
            unit = jnp.where(lane < k, pivot[j], jnp.where(lane == k + j, 1.0, 0.0))
            for i in range(j):
                unit = unit - ratio[j][i] * solved[i]
            solved.append(unit)
            put(k + j, (unit * lax.rsqrt(entry[j][j]))[:1])
        if k + STEP == size:
            break
        front = [jnp.where(lane == k + j, pivot[j] + 1.0, pivot[j]) for j in span]
        for j in span:
            for i in range(j):
                front[j] = front[j] - ratio[j][i] * front[i]
        back = [front[j] * inverse[j] for j in span]
        for j in reversed(span):
            for i in range(j + 1, STEP):
                back[j] = back[j] - ratio[i][j] * back[i]
        for g in range((k + STEP) // 8, groups):
            change = None
            for j in span:
                term = jnp.broadcast_to(rows[g][:, k + j : k + j + 1], (8, size)) * back[j]
                change = term if change is None else change + term
            if g == group:
                change = jnp.where(down < inside + STEP, 0.0, change)
            rows[g] = rows[g] - change


def both_grams(info_ref, own_ref, other_ref, other_start, edge):
    own, other = take_block(own_ref, edge), take_block(other_ref, edge, other_start)
    first = info_ref[2] == 0
    return jnp.where(first, own, other), jnp.where(first, other, own)


def factor_kernel(start, info_ref, own_ref, other_ref, pair_ref, out_ref):
    edge = out_ref.shape[0] // 2
    gram_00, gram_11 = both_grams(info_ref, own_ref, other_ref, start, edge)
    cross = take_block(pair_ref, edge)
    cross = jnp.where(info_ref[2] == 0, cross, cross.T)
    upper = jnp.concatenate([gram_00, cross.T], axis=1)
    lower = jnp.concatenate([cross, gram_11], axis=1)

    def put(index, row):
        out_ref[index : index + 1] = row

    inverse_factor(jnp.concatenate([upper, lower], axis=0), put)


def final_kernel(pieces, edge, info_ref, inverse_ref, *refs):
    own_refs, other_refs, (out_ref, held, sems) = refs[:pieces], refs[pieces : 2 * pieces], refs[2 * pieces :]
    width = own_refs[0].shape[1]
    inverse = inverse_ref[...]
    first = info_ref[2] == 0
    left, right = inverse[:, :edge], inverse[:, edge:]
    inverse = jnp.concatenate([jnp.where(first, left, right), jnp.where(first, right, left)], axis=1)
    inverse_high, inverse_low = split(inverse)
    both = jnp.concatenate([inverse_high, inverse_low], axis=0)
    row = lax.broadcasted_iota(jnp.int32, (2 * edge, width), 0)
    lane = lax.broadcasted_iota(jnp.int32, (2 * edge, width), 1)
    copies = []
    for near in range(pieces):
        part = jnp.concatenate([own_refs[near][:edge], other_refs[near][:edge]], axis=0)
        part_high, part_low = split(part)
        product = jnp.dot(both, part_high, preferred_element_type=F32)
        small = jnp.dot(inverse_high, part_low, preferred_element_type=F32)
        product = product[: 2 * edge] + (product[2 * edge :] + small)
        place = jnp.bitwise_xor(info_ref[0], near)
        place_lane = lane + place * width
        early = (place_lane < edge) & (place_lane + info_ref[3] * edge < row)
        held[near] = jnp.where(early, 0.0, product)
        copy = pltpu.make_async_copy(
            held.at[near],
            out_ref.at[0, :, pl.ds(pl.multiple_of(place * width, width), width)],
            sems.at[near],
        )
        copy.start()
        copies.append(copy)
    for copy in copies:
        copy.wait()


def vmem():
    return pl.BlockSpec(memory_space=pltpu.VMEM)


def smem():
    return pl.BlockSpec(memory_space=pltpu.SMEM)


def per_device(child_tiles, block_mask, destination):
    tile_count, edge, columns = child_tiles.shape
    rows = tile_count * edge
    row_count, col_count = lax.axis_size("row"), lax.axis_size("col")
    bits = row_count.bit_length() - 1
    split_bits = min(2, bits - 1, (columns // 128).bit_length() - 1)
    pieces = 1 << split_bits
    width = columns // pieces
    row, leaf, col = lax.axis_index("row"), lax.axis_index("leaf"), lax.axis_index("col")
    own_panel = col if col_count == PANELS else jnp.zeros_like(col)
    info = jnp.stack([row % pieces, leaf, own_panel, col]).astype(jnp.int32)
    params = pltpu.CompilerParams(vmem_limit_bytes=VMEM_LIMIT)
    wide_params = pltpu.CompilerParams(vmem_limit_bytes=OWN_VMEM_LIMIT)

    blocks = columns // edge
    mask_tile = jnp.pad(block_mask.astype(F32), ((0, edge - tile_count), (0, edge - blocks)))[None]
    lead, mask = pl.pallas_call(
        prep_kernel,
        out_shape=(jax.ShapeDtypeStruct((edge, rows), F32), jax.ShapeDtypeStruct((tile_count, blocks), F32)),
        in_specs=[vmem()],
        out_specs=(vmem(), vmem()),
        compiler_params=params,
        name="lead_prep",
    )(jnp.concatenate([child_tiles[:, :, :edge], mask_tile], axis=0))

    if col_count == PANELS:
        lead_own = lead
        lead_other = lax.ppermute(lead, "col", [(i, 1 - i) for i in range(PANELS)])
    else:
        gathered = lax.all_gather(lead, "col")
        lead_own, lead_other = gathered[0], gathered[1]

    swap = col_count == PANELS
    gram_rows = edge * edge // width
    factor = pltpu.VMEM((4 * edge, rows), BF16)
    work = pl.CostEstimate(flops=12 * edge * rows * columns, bytes_accessed=4 * rows * columns, transcendentals=0)

    def sums(extra):
        return jax.ShapeDtypeStruct((pieces, edge + extra, width), F32)

    halves = jax.ShapeDtypeStruct((rows, columns), BF16)
    keep, send, high, low, mine = pl.pallas_call(
        functools.partial(own_kernel, row_count),
        out_shape=(sums(gram_rows), sums(gram_rows), halves, halves, jax.ShapeDtypeStruct((1, rows), F32)),
        in_specs=[smem(), smem(), vmem(), vmem(), pl.BlockSpec(memory_space=pl.ANY)],
        out_specs=(vmem(),) * 5,
        scratch_shapes=[
            factor,
            pltpu.VMEM((tile_count, edge, columns), F32),
            pltpu.VMEM((tile_count, columns), F32),
            pltpu.VMEM((2 * edge, columns), F32),
            pltpu.SemaphoreType.DMA((tile_count,)),
        ],
        compiler_params=wide_params,
        cost_estimate=work,
        name="panel_own",
    )(info, destination.reshape(1, tile_count), mask, lead_own, child_tiles)

    def over_leaf(keep, send):
        return keep + lax.ppermute(send, "leaf", [(0, 1), (1, 0)])

    def over_row(value, bit):
        return lax.ppermute(value, "row", [(i, i ^ bit) for i in range(row_count)])

    def reduce_near(partial, order):
        total = partial[0]
        for near in order:
            total = lax.optimization_barrier(total + over_row(partial[near], near))
        return total

    def reduce_far(total):
        for bit in range(split_bits, bits):
            total = total + over_row(total, 1 << bit)
        return total

    def gather_pieces(total):
        return [total[:edge]] + [over_row(total[:edge], near) for near in range(1, pieces)]

    send, lead_other = lax.optimization_barrier((send, lead_other))
    own_sum = reduce_far(reduce_near(over_leaf(keep, send), range(1, pieces)))
    own_pieces = gather_pieces(own_sum)

    pair_rows = gram_rows if swap else 2 * gram_rows
    keep, send = pl.pallas_call(
        functools.partial(pair_kernel, not swap),
        out_shape=(sums(pair_rows), sums(pair_rows)),
        in_specs=[smem(), vmem(), vmem(), vmem(), vmem(), vmem()],
        out_specs=(vmem(),) * 2,
        scratch_shapes=[factor],
        compiler_params=params,
        cost_estimate=work,
        name="panel_pair",
    )(info, mine, lead_other, lead_own, high, low)
    other_sum = reduce_far(reduce_near(over_leaf(keep, send), range(1, pieces)))

    other_pieces = gather_pieces(other_sum)
    own_gram, pair_gram = own_sum[edge:], other_sum[edge:]
    if swap:
        other_gram, start = lax.ppermute(own_gram, "col", [(i, 1 - i) for i in range(PANELS)]), 0
    else:
        other_gram, start = pair_gram, edge // 16
    inverse = pl.pallas_call(
        functools.partial(factor_kernel, start),
        out_shape=jax.ShapeDtypeStruct((2 * edge, 2 * edge), F32),
        in_specs=[smem()] + [vmem()] * 3,
        out_specs=vmem(),
        compiler_params=params,
        name="gram_factor",
    )(info, own_gram, other_gram, pair_gram)

    return pl.pallas_call(
        functools.partial(final_kernel, pieces, edge),
        out_shape=jax.ShapeDtypeStruct((1, 2 * edge, columns), F32),
        in_specs=[smem(), vmem()] + [vmem()] * (2 * pieces),
        out_specs=pl.BlockSpec(memory_space=pl.ANY),
        scratch_shapes=[pltpu.VMEM((pieces, 2 * edge, width), F32), pltpu.SemaphoreType.DMA((pieces,))],
        compiler_params=params,
        name="apply_inverse",
    )(info, inverse, *own_pieces, *other_pieces)


def solution(mesh):
    in_specs = (
        P(("leaf", "row"), None, "col"),
        P(("leaf", "row"), "col"),
        P(("leaf", "row"), None),
    )
    out_specs = P("leaf", None, "col")
    return jax.shard_map(per_device, mesh=mesh, in_specs=in_specs, out_specs=out_specs, check_vma=False)
```

```python
import functools

import jax
import jax.numpy as jnp
from jax import lax
from jax.experimental import pallas as pl
from jax.experimental.pallas import tpu as pltpu
from jax.sharding import PartitionSpec as P

PANELS = 2
VMEM_LIMIT = 16 * 1024 * 1024
OWN_VMEM_LIMIT = 44 * 1024 * 1024
F32 = jnp.float32
BF16 = jnp.bfloat16
HIGHEST = lax.Precision.HIGHEST


def split(value):
    high = value.astype(BF16)
    return high, (value - high.astype(F32)).astype(BF16)


def dot_nt(a, b):
    return lax.dot_general(a, b, (((1,), (1,)), ((), ())), precision=HIGHEST, preferred_element_type=F32)


def prep_kernel(lead_ref, flipped_ref, mask_ref):
    edge = flipped_ref.shape[0]
    tile_count, blocks = mask_ref.shape
    mask = lead_ref[tile_count, :tile_count, :blocks]
    mask_ref[...] = mask
    flipped_ref[...] = (lead_ref[:tile_count] * mask[:, :1].reshape(tile_count, 1, 1)).reshape(-1, edge).T


def spread_mask(mask, columns, edge):
    blocks = mask.shape[1]
    over = lax.broadcasted_iota(jnp.int32, (blocks, columns), 1) // edge
    over = (over == lax.broadcasted_iota(jnp.int32, (blocks, columns), 0)).astype(F32)
    return jnp.dot(mask, over, preferred_element_type=F32)


def spread_front(dest_ref, leaf, per_front, rows):
    tile_count = dest_ref.shape[1]
    place = lax.broadcasted_iota(jnp.int32, (1, rows), 1) // (rows // tile_count)
    mine = jnp.zeros((1, rows), F32)
    for tile in range(tile_count):
        here = (dest_ref[0, tile] // per_front == leaf).astype(F32)
        mine = jnp.where(place == tile, here, mine)
    return mine


def by_front(lead, mine):
    return lead * mine, lead * (1.0 - mine)


def fill_factor(lhs, kept, sent, edge):
    for place, part in enumerate((kept, sent)):
        part_high, part_low = split(part)
        lhs[place * edge : (place + 1) * edge] = part_high
        lhs[(place + 2) * edge : (place + 3) * edge] = part_low


def panel_product(lhs, high, low, edge):
    big = jnp.dot(lhs, high, preferred_element_type=F32)
    small = jnp.dot(lhs[: 2 * edge], low, preferred_element_type=F32)
    return big[: 2 * edge] + (big[2 * edge :] + small)


def put_gram(blocks, out, edge):
    for near in range(out.shape[0]):
        place_slabs(blocks, out.at[near, edge:])


def halves_beside(block):
    return jnp.concatenate([block[: block.shape[0] // 2], block[block.shape[0] // 2 :]], axis=1)


def own_kernel(per_front, info_ref, dest_ref, mask_ref, lead_ref, tiles_ref, keep_ref, send_ref, high, low, mine_ref, lhs, held, wide_ref, total_ref, sems):
    tile_count, edge, columns = held.shape
    pieces, _, width = keep_ref.shape
    copies = [pltpu.make_async_copy(tiles_ref.at[tile], held.at[tile], sems.at[tile]) for tile in range(tile_count)]
    for copy in copies:
        copy.start()
    wide_ref[...] = spread_mask(mask_ref[...], columns, edge)
    mine_ref[...] = spread_front(dest_ref, info_ref[1], per_front, lead_ref.shape[1])
    lead = lead_ref[...]
    parts = by_front(lead, mine_ref[...])
    fill_factor(lhs, *parts, edge)
    gram = dot_nt(jnp.concatenate(parts, axis=0), lead)
    put_gram(halves_beside(gram[:edge]), keep_ref, edge)
    put_gram(halves_beside(gram[edge:]), send_ref, edge)
    group = max(1, 256 // edge)
    for first in range(0, tile_count, group):
        for tile in range(first, first + group):
            copies[tile].wait()
            value = held[tile] * wide_ref[tile : tile + 1, :]
            value_high, value_low = split(value)
            high[tile * edge : (tile + 1) * edge] = value_high
            low[tile * edge : (tile + 1) * edge] = value_low
        deep = slice(first * edge, (first + group) * edge)
        for piece in range(pieces):
            here = slice(piece * width, (piece + 1) * width)
            part = panel_product(lhs[:, deep], high[deep, here], low[deep, here], edge)
            if first + group < tile_count:
                total_ref[:, here] = part if first == 0 else total_ref[:, here] + part
                continue
            total = total_ref[:, here] + part if first else part
            near = jnp.bitwise_xor(info_ref[0], piece)
            keep_ref[near, :edge] = total[:edge]
            send_ref[near, :edge] = total[edge:]


def pair_kernel(with_other, info_ref, mine_ref, lead_ref, own_ref, high, low, keep_ref, send_ref, lhs):
    edge = lead_ref.shape[0]
    pieces, _, width = keep_ref.shape
    lead, own = lead_ref[...], own_ref[...]
    parts = by_front(lead, mine_ref[...])
    fill_factor(lhs, *parts, edge)
    both = jnp.concatenate(parts, axis=0)
    cross = dot_nt(both, own)
    other = dot_nt(both, lead) if with_other else None
    for place, out in enumerate((keep_ref, send_ref)):
        here = slice(place * edge, (place + 1) * edge)
        blocks = halves_beside(cross[here])
        if with_other:
            blocks = jnp.concatenate([blocks, halves_beside(other[here])], axis=0)
        put_gram(blocks, out, edge)
    for piece in range(pieces):
        here = slice(piece * width, (piece + 1) * width)
        total = panel_product(lhs[...], high[:, here], low[:, here], edge)
        near = jnp.bitwise_xor(info_ref[0], piece)
        keep_ref[near, :edge] = total[:edge]
        send_ref[near, :edge] = total[edge:]


def place_slabs(value, out):
    across = out.shape[1] // value.shape[1]
    for slab in range(value.shape[0] // 8):
        down, right = slab // across, slab % across
        out[down * 8 : (down + 1) * 8, right * 128 : (right + 1) * 128] = value[slab * 8 : (slab + 1) * 8]


def take_block(ref, edge, start=0):
    across = ref.shape[1] // 128
    slabs = []
    for slab in range(start, start + edge // 16):
        down, right = slab // across, slab % across
        slabs.append(ref[down * 8 : (down + 1) * 8, right * 128 : (right + 1) * 128])
    value = jnp.concatenate(slabs, axis=0)
    return jnp.concatenate([value[:, :edge], value[:, edge:]], axis=0)


STEP = 8


def inverse_factor(whole, put):
    size = whole.shape[0]
    groups = size // 8
    rows = [whole[8 * i : 8 * i + 8] for i in range(groups)]
    lane = lax.broadcasted_iota(jnp.int32, (8, size), 1)
    down = lax.broadcasted_iota(jnp.int32, (8, size), 0)
    span = range(STEP)
    for k in range(0, size, STEP):
        group, inside = k // 8, k % 8
        pivot = [jnp.broadcast_to(rows[group][inside + j : inside + j + 1], (8, size)) for j in span]
        entry = [[jnp.broadcast_to(pivot[i][:, k + j : k + j + 1], (8, size)) for j in range(i + 1)] for i in span]
        ratio = [[None] * STEP for _ in span]
        inverse = [None] * STEP
        for j in span:
            inverse[j] = 1.0 / entry[j][j]
            for i in range(j + 1, STEP):
                ratio[i][j] = entry[i][j] * inverse[j]
            for i in range(j + 1, STEP):
                for m in range(j + 1, i + 1):
                    entry[i][m] = entry[i][m] - entry[i][j] * entry[m][j] * inverse[j]
        solved = []
        for j in span:
            unit = jnp.where(lane < k, pivot[j], jnp.where(lane == k + j, 1.0, 0.0))
            for i in range(j):
                unit = unit - ratio[j][i] * solved[i]
            solved.append(unit)
            put(k + j, (unit * lax.rsqrt(entry[j][j]))[:1])
        if k + STEP == size:
            break
        front = [jnp.where(lane == k + j, pivot[j] + 1.0, pivot[j]) for j in span]
        for j in span:
            for i in range(j):
                front[j] = front[j] - ratio[j][i] * front[i]
        back = [front[j] * inverse[j] for j in span]
        for j in reversed(span):
            for i in reversed(range(j + 1, STEP)):
                back[j] = back[j] - ratio[i][j] * back[i]
        for g in range((k + STEP) // 8, groups):
            row = rows[g]
            for j in reversed(span):
                row = row - jnp.broadcast_to(rows[g][:, k + j : k + j + 1], (8, size)) * back[j]
            rows[g] = jnp.where(down < inside + STEP, rows[g], row) if g == group else row


def both_grams(info_ref, own_ref, other_ref, other_start, edge):
    own, other = take_block(own_ref, edge), take_block(other_ref, edge, other_start)
    first = info_ref[2] == 0
    return jnp.where(first, own, other), jnp.where(first, other, own)


def factor_kernel(start, info_ref, own_ref, other_ref, pair_ref, out_ref):
    edge = out_ref.shape[0] // 2
    gram_00, gram_11 = both_grams(info_ref, own_ref, other_ref, start, edge)
    cross = take_block(pair_ref, edge)
    cross = jnp.where(info_ref[2] == 0, cross, cross.T)
    upper = jnp.concatenate([gram_00, cross.T], axis=1)
    lower = jnp.concatenate([cross, gram_11], axis=1)

    def put(index, row):
        out_ref[index : index + 1] = row

    inverse_factor(jnp.concatenate([upper, lower], axis=0), put)


def final_kernel(pieces, edge, info_ref, inverse_ref, *refs):
    own_refs, other_refs, (out_ref, held, sems) = refs[:pieces], refs[pieces : 2 * pieces], refs[2 * pieces :]
    width = own_refs[0].shape[1]
    inverse = inverse_ref[...]
    first = info_ref[2] == 0
    left, right = inverse[:, :edge], inverse[:, edge:]
    inverse = jnp.concatenate([jnp.where(first, left, right), jnp.where(first, right, left)], axis=1)
    inverse_high, inverse_low = split(inverse)
    both = jnp.concatenate([inverse_high, inverse_low], axis=0)
    row = lax.broadcasted_iota(jnp.int32, (2 * edge, width), 0)
    lane = lax.broadcasted_iota(jnp.int32, (2 * edge, width), 1)
    copies = []
    for near in range(pieces):
        part = jnp.concatenate([own_refs[near][:edge], other_refs[near][:edge]], axis=0)
        part_high, part_low = split(part)
        product = jnp.dot(both, part_high, preferred_element_type=F32)
        small = jnp.dot(inverse_high, part_low, preferred_element_type=F32)
        product = product[: 2 * edge] + (product[2 * edge :] + small)
        place = jnp.bitwise_xor(info_ref[0], near)
        place_lane = lane + place * width
        early = (place_lane < edge) & (place_lane + info_ref[3] * edge < row)
        held[near] = jnp.where(early, 0.0, product)
        copy = pltpu.make_async_copy(
            held.at[near],
            out_ref.at[0, :, pl.ds(pl.multiple_of(place * width, width), width)],
            sems.at[near],
        )
        copy.start()
        copies.append(copy)
    for copy in copies:
        copy.wait()


def vmem():
    return pl.BlockSpec(memory_space=pltpu.VMEM)


def smem():
    return pl.BlockSpec(memory_space=pltpu.SMEM)


def per_device(child_tiles, block_mask, destination):
    tile_count, edge, columns = child_tiles.shape
    rows = tile_count * edge
    row_count, col_count = lax.axis_size("row"), lax.axis_size("col")
    bits = row_count.bit_length() - 1
    split_bits = min(2, bits - 1, (columns // 128).bit_length() - 1)
    pieces = 1 << split_bits
    width = columns // pieces
    row, leaf, col = lax.axis_index("row"), lax.axis_index("leaf"), lax.axis_index("col")
    own_panel = col if col_count == PANELS else jnp.zeros_like(col)
    info = jnp.stack([row % pieces, leaf, own_panel, col]).astype(jnp.int32)
    params = pltpu.CompilerParams(vmem_limit_bytes=VMEM_LIMIT)
    wide_params = pltpu.CompilerParams(vmem_limit_bytes=OWN_VMEM_LIMIT)

    blocks = columns // edge
    mask_tile = jnp.pad(block_mask.astype(F32), ((0, edge - tile_count), (0, edge - blocks)))[None]
    lead, mask = pl.pallas_call(
        prep_kernel,
        out_shape=(jax.ShapeDtypeStruct((edge, rows), F32), jax.ShapeDtypeStruct((tile_count, blocks), F32)),
        in_specs=[vmem()],
        out_specs=(vmem(), vmem()),
        compiler_params=params,
        name="lead_prep",
    )(jnp.concatenate([child_tiles[:, :, :edge], mask_tile], axis=0))

    if col_count == PANELS:
        lead_own = lead
        lead_other = lax.ppermute(lead, "col", [(i, 1 - i) for i in range(PANELS)])
    else:
        gathered = lax.all_gather(lead, "col")
        lead_own, lead_other = gathered[0], gathered[1]

    swap = col_count == PANELS
    gram_rows = edge * edge // width
    factor = pltpu.VMEM((4 * edge, rows), BF16)
    work = pl.CostEstimate(flops=12 * edge * rows * columns, bytes_accessed=4 * rows * columns, transcendentals=0)

    def sums(extra):
        return jax.ShapeDtypeStruct((pieces, edge + extra, width), F32)

    halves = jax.ShapeDtypeStruct((rows, columns), BF16)
    keep, send, high, low, mine = pl.pallas_call(
        functools.partial(own_kernel, row_count),
        out_shape=(sums(gram_rows), sums(gram_rows), halves, halves, jax.ShapeDtypeStruct((1, rows), F32)),
        in_specs=[smem(), smem(), vmem(), vmem(), pl.BlockSpec(memory_space=pl.ANY)],
        out_specs=(vmem(),) * 5,
        scratch_shapes=[
            factor,
            pltpu.VMEM((tile_count, edge, columns), F32),
            pltpu.VMEM((tile_count, columns), F32),
            pltpu.VMEM((2 * edge, columns), F32),
            pltpu.SemaphoreType.DMA((tile_count,)),
        ],
        compiler_params=wide_params,
        cost_estimate=work,
        name="panel_own",
    )(info, destination.reshape(1, tile_count), mask, lead_own, child_tiles)

    def over_leaf(keep, send):
        return keep + lax.ppermute(send, "leaf", [(0, 1), (1, 0)])

    def over_row(value, bit):
        return lax.ppermute(value, "row", [(i, i ^ bit) for i in range(row_count)])

    def reduce_near(partial, order):
        total = partial[0]
        for near in order:
            total = lax.optimization_barrier(total + over_row(partial[near], near))
        return total

    def reduce_far(total):
        for bit in range(split_bits, bits):
            total = total + over_row(total, 1 << bit)
        return total

    def gather_pieces(total):
        return [total[:edge]] + [over_row(total[:edge], near) for near in range(1, pieces)]

    send, lead_other = lax.optimization_barrier((send, lead_other))
    own_sum = reduce_far(reduce_near(over_leaf(keep, send), range(1, pieces)))
    own_pieces = gather_pieces(own_sum)

    pair_rows = gram_rows if swap else 2 * gram_rows
    keep, send = pl.pallas_call(
        functools.partial(pair_kernel, not swap),
        out_shape=(sums(pair_rows), sums(pair_rows)),
        in_specs=[smem(), vmem(), vmem(), vmem(), vmem(), vmem()],
        out_specs=(vmem(),) * 2,
        scratch_shapes=[factor],
        compiler_params=params,
        cost_estimate=work,
        name="panel_pair",
    )(info, mine, lead_other, lead_own, high, low)
    other_sum = reduce_far(reduce_near(over_leaf(keep, send), range(1, pieces)))

    other_pieces = gather_pieces(other_sum)
    own_gram, pair_gram = own_sum[edge:], other_sum[edge:]
    if swap:
        other_gram, start = lax.ppermute(own_gram, "col", [(i, 1 - i) for i in range(PANELS)]), 0
    else:
        other_gram, start = pair_gram, edge // 16
    inverse = pl.pallas_call(
        functools.partial(factor_kernel, start),
        out_shape=jax.ShapeDtypeStruct((2 * edge, 2 * edge), F32),
        in_specs=[smem()] + [vmem()] * 3,
        out_specs=vmem(),
        compiler_params=params,
        name="gram_factor",
    )(info, own_gram, other_gram, pair_gram)

    return pl.pallas_call(
        functools.partial(final_kernel, pieces, edge),
        out_shape=jax.ShapeDtypeStruct((1, 2 * edge, columns), F32),
        in_specs=[smem(), vmem()] + [vmem()] * (2 * pieces),
        out_specs=pl.BlockSpec(memory_space=pl.ANY),
        scratch_shapes=[pltpu.VMEM((pieces, 2 * edge, width), F32), pltpu.SemaphoreType.DMA((pieces,))],
        compiler_params=params,
        name="apply_inverse",
    )(info, inverse, *own_pieces, *other_pieces)


def solution(mesh):
    in_specs = (
        P(("leaf", "row"), None, "col"),
        P(("leaf", "row"), "col"),
        P(("leaf", "row"), None),
    )
    out_specs = P("leaf", None, "col")
    return jax.shard_map(per_device, mesh=mesh, in_specs=in_specs, out_specs=out_specs, check_vma=False)
```

```python
import functools

import jax
import jax.numpy as jnp
from jax import lax
from jax.experimental import pallas as pl
from jax.experimental.pallas import tpu as pltpu
from jax.sharding import PartitionSpec as P

PANELS = 2
VMEM_LIMIT = 16 * 1024 * 1024
OWN_VMEM_LIMIT = 44 * 1024 * 1024
F32 = jnp.float32
BF16 = jnp.bfloat16
HIGHEST = lax.Precision.HIGHEST


def split(value):
    high = value.astype(BF16)
    return high, (value - high.astype(F32)).astype(BF16)


def dot_nt(a, b):
    return lax.dot_general(a, b, (((1,), (1,)), ((), ())), precision=HIGHEST, preferred_element_type=F32)


def prep_kernel(lead_ref, flipped_ref, mask_ref):
    edge = flipped_ref.shape[0]
    tile_count, blocks = mask_ref.shape
    mask = lead_ref[tile_count, :tile_count, :blocks]
    mask_ref[...] = mask
    flipped_ref[...] = (lead_ref[:tile_count] * mask[:, :1].reshape(tile_count, 1, 1)).reshape(-1, edge).T


def spread_mask(mask, columns, edge):
    blocks = mask.shape[1]
    over = lax.broadcasted_iota(jnp.int32, (blocks, columns), 1) // edge
    over = (over == lax.broadcasted_iota(jnp.int32, (blocks, columns), 0)).astype(F32)
    return jnp.dot(mask, over, preferred_element_type=F32)


def spread_front(dest_ref, leaf, per_front, rows):
    tile_count = dest_ref.shape[1]
    place = lax.broadcasted_iota(jnp.int32, (1, rows), 1) // (rows // tile_count)
    mine = jnp.zeros((1, rows), F32)
    for tile in range(tile_count):
        here = (dest_ref[0, tile] // per_front == leaf).astype(F32)
        mine = jnp.where(place == tile, here, mine)
    return mine


def by_front(lead, mine):
    return lead * mine, lead * (1.0 - mine)


def fill_factor(lhs, kept, sent, edge):
    for place, part in enumerate((kept, sent)):
        part_high, part_low = split(part)
        lhs[place * edge : (place + 1) * edge] = part_high
        lhs[(place + 2) * edge : (place + 3) * edge] = part_low


def panel_product(lhs, high, low, edge):
    big = jnp.dot(lhs, high, preferred_element_type=F32)
    small = jnp.dot(lhs[: 2 * edge], low, preferred_element_type=F32)
    return big[: 2 * edge] + (big[2 * edge :] + small)


def put_gram(blocks, out, edge):
    for near in range(out.shape[0]):
        place_slabs(blocks, out.at[near, edge:])


def halves_beside(block):
    return jnp.concatenate([block[: block.shape[0] // 2], block[block.shape[0] // 2 :]], axis=1)


def own_kernel(per_front, info_ref, dest_ref, mask_ref, lead_ref, tiles_ref, keep_ref, send_ref, high, low, mine_ref, lhs, held, wide_ref, total_ref, sems):
    tile_count, edge, columns = held.shape
    pieces, _, width = keep_ref.shape
    copies = [pltpu.make_async_copy(tiles_ref.at[tile], held.at[tile], sems.at[tile]) for tile in range(tile_count)]
    for copy in copies:
        copy.start()
    wide_ref[...] = spread_mask(mask_ref[...], columns, edge)
    mine_ref[...] = spread_front(dest_ref, info_ref[1], per_front, lead_ref.shape[1])
    lead = lead_ref[...]
    parts = by_front(lead, mine_ref[...])
    fill_factor(lhs, *parts, edge)
    gram = dot_nt(jnp.concatenate(parts, axis=0), lead)
    put_gram(halves_beside(gram[:edge]), keep_ref, edge)
    put_gram(halves_beside(gram[edge:]), send_ref, edge)
    group = max(1, 256 // edge)
    for first in range(0, tile_count, group):
        for tile in range(first, first + group):
            copies[tile].wait()
            value = held[tile] * wide_ref[tile : tile + 1, :]
            value_high, value_low = split(value)
            high[tile * edge : (tile + 1) * edge] = value_high
            low[tile * edge : (tile + 1) * edge] = value_low
        deep = slice(first * edge, (first + group) * edge)
        for piece in range(pieces):
            here = slice(piece * width, (piece + 1) * width)
            part = panel_product(lhs[:, deep], high[deep, here], low[deep, here], edge)
            if first + group < tile_count:
                total_ref[:, here] = part if first == 0 else total_ref[:, here] + part
                continue
            total = total_ref[:, here] + part if first else part
            near = jnp.bitwise_xor(info_ref[0], piece)
            keep_ref[near, :edge] = total[:edge]
            send_ref[near, :edge] = total[edge:]


def pair_kernel(with_other, info_ref, mine_ref, lead_ref, own_ref, high, low, keep_ref, send_ref, lhs):
    edge = lead_ref.shape[0]
    pieces, _, width = keep_ref.shape
    lead, own = lead_ref[...], own_ref[...]
    parts = by_front(lead, mine_ref[...])
    fill_factor(lhs, *parts, edge)
    both = jnp.concatenate(parts, axis=0)
    cross = dot_nt(both, own)
    other = dot_nt(both, lead) if with_other else None
    for place, out in enumerate((keep_ref, send_ref)):
        here = slice(place * edge, (place + 1) * edge)
        blocks = halves_beside(cross[here])
        if with_other:
            blocks = jnp.concatenate([blocks, halves_beside(other[here])], axis=0)
        put_gram(blocks, out, edge)
    for piece in range(pieces):
        here = slice(piece * width, (piece + 1) * width)
        total = panel_product(lhs[...], high[:, here], low[:, here], edge)
        near = jnp.bitwise_xor(info_ref[0], piece)
        keep_ref[near, :edge] = total[:edge]
        send_ref[near, :edge] = total[edge:]


def place_slabs(value, out):
    across = out.shape[1] // value.shape[1]
    for slab in range(value.shape[0] // 8):
        down, right = slab // across, slab % across
        out[down * 8 : (down + 1) * 8, right * 128 : (right + 1) * 128] = value[slab * 8 : (slab + 1) * 8]


def take_block(ref, edge, start=0):
    across = ref.shape[1] // 128
    slabs = []
    for slab in range(start, start + edge // 16):
        down, right = slab // across, slab % across
        slabs.append(ref[down * 8 : (down + 1) * 8, right * 128 : (right + 1) * 128])
    value = jnp.concatenate(slabs, axis=0)
    return jnp.concatenate([value[:, :edge], value[:, edge:]], axis=0)


STEP = 8


def inverse_factor(whole, put):
    size = whole.shape[0]
    groups = size // 8
    rows = [whole[8 * i : 8 * i + 8] for i in range(groups)]
    lane = lax.broadcasted_iota(jnp.int32, (8, size), 1)
    down = lax.broadcasted_iota(jnp.int32, (8, size), 0)
    span = range(STEP)
    for k in range(0, size, STEP):
        group, inside = k // 8, k % 8
        pivot = [jnp.broadcast_to(rows[group][inside + j : inside + j + 1], (8, size)) for j in span]
        entry = [[jnp.broadcast_to(pivot[i][:, k + j : k + j + 1], (8, size)) for j in range(i + 1)] for i in span]
        ratio = [[None] * STEP for _ in span]
        inverse = [None] * STEP
        for j in span:
            inverse[j] = 1.0 / entry[j][j]
            for i in range(j + 1, STEP):
                ratio[i][j] = entry[i][j] * inverse[j]
            for i in range(j + 1, STEP):
                for m in range(j + 1, i + 1):
                    entry[i][m] = entry[i][m] - entry[i][j] * entry[m][j] * inverse[j]
        solved = []
        for j in span:
            unit = jnp.where(lane < k, pivot[j], jnp.where(lane == k + j, 1.0, 0.0))
            for i in range(j):
                unit = unit - ratio[j][i] * solved[i]
            solved.append(unit)
            put(k + j, (unit * lax.rsqrt(entry[j][j]))[:1])
        if k + STEP == size:
            break
        front = [jnp.where(lane == k + j, pivot[j] + 1.0, pivot[j]) for j in span]
        for j in span:
            for i in range(j):
                front[j] = front[j] - ratio[j][i] * front[i]
        back = [front[j] * inverse[j] for j in span]
        for j in reversed(span):
            for i in reversed(range(j + 1, STEP)):
                back[j] = back[j] - ratio[i][j] * back[i]
        for g in range((k + STEP) // 8, groups):
            row = rows[g]
            for j in reversed(span):
                row = row - jnp.broadcast_to(rows[g][:, k + j : k + j + 1], (8, size)) * back[j]
            rows[g] = jnp.where(down < inside + STEP, rows[g], row) if g == group else row


def both_grams(info_ref, own_ref, other_ref, other_start, edge):
    own, other = take_block(own_ref, edge), take_block(other_ref, edge, other_start)
    first = info_ref[2] == 0
    return jnp.where(first, own, other), jnp.where(first, other, own)


def factor_kernel(start, info_ref, own_ref, other_ref, pair_ref, out_ref):
    edge = out_ref.shape[0] // 2
    gram_00, gram_11 = both_grams(info_ref, own_ref, other_ref, start, edge)
    cross = take_block(pair_ref, edge)
    cross = jnp.where(info_ref[2] == 0, cross, cross.T)
    upper = jnp.concatenate([gram_00, cross.T], axis=1)
    lower = jnp.concatenate([cross, gram_11], axis=1)

    def put(index, row):
        out_ref[index : index + 1] = row

    inverse_factor(jnp.concatenate([upper, lower], axis=0), put)


def final_kernel(pieces, edge, info_ref, inverse_ref, *refs):
    own_refs, other_refs, (out_ref, held, sems) = refs[:pieces], refs[pieces : 2 * pieces], refs[2 * pieces :]
    width = own_refs[0].shape[1]
    inverse = inverse_ref[...]
    first = info_ref[2] == 0
    left, right = inverse[:, :edge], inverse[:, edge:]
    inverse = jnp.concatenate([jnp.where(first, left, right), jnp.where(first, right, left)], axis=1)
    inverse_high, inverse_low = split(inverse)
    both = jnp.concatenate([inverse_high, inverse_low], axis=0)
    row = lax.broadcasted_iota(jnp.int32, (2 * edge, width), 0)
    lane = lax.broadcasted_iota(jnp.int32, (2 * edge, width), 1)
    copies = []
    for near in range(pieces):
        part = jnp.concatenate([own_refs[near][:edge], other_refs[near][:edge]], axis=0)
        part_high, part_low = split(part)
        product = jnp.dot(both, part_high, preferred_element_type=F32)
        small = jnp.dot(inverse_high, part_low, preferred_element_type=F32)
        product = product[: 2 * edge] + (product[2 * edge :] + small)
        place = jnp.bitwise_xor(info_ref[0], near)
        place_lane = lane + place * width
        early = (place_lane < edge) & (place_lane + info_ref[3] * edge < row)
        held[near] = jnp.where(early, 0.0, product)
        copy = pltpu.make_async_copy(
            held.at[near],
            out_ref.at[0, :, pl.ds(pl.multiple_of(place * width, width), width)],
            sems.at[near],
        )
        copy.start()
        copies.append(copy)
    for copy in copies:
        copy.wait()


def vmem():
    return pl.BlockSpec(memory_space=pltpu.VMEM)


def smem():
    return pl.BlockSpec(memory_space=pltpu.SMEM)


def per_device(child_tiles, block_mask, destination):
    tile_count, edge, columns = child_tiles.shape
    rows = tile_count * edge
    row_count, col_count = lax.axis_size("row"), lax.axis_size("col")
    bits = row_count.bit_length() - 1
    split_bits = min(2, bits - 1, (columns // 128).bit_length() - 1)
    pieces = 1 << split_bits
    width = columns // pieces
    row, leaf, col = lax.axis_index("row"), lax.axis_index("leaf"), lax.axis_index("col")
    own_panel = col if col_count == PANELS else jnp.zeros_like(col)
    mirror = pieces // 2
    piece = row % pieces ^ (row // pieces % 2 * mirror)
    info = jnp.stack([piece, leaf, own_panel, col]).astype(jnp.int32)
    params = pltpu.CompilerParams(vmem_limit_bytes=VMEM_LIMIT)
    wide_params = pltpu.CompilerParams(vmem_limit_bytes=OWN_VMEM_LIMIT)

    blocks = columns // edge
    mask_tile = jnp.pad(block_mask.astype(F32), ((0, edge - tile_count), (0, edge - blocks)))[None]
    lead, mask = pl.pallas_call(
        prep_kernel,
        out_shape=(jax.ShapeDtypeStruct((edge, rows), F32), jax.ShapeDtypeStruct((tile_count, blocks), F32)),
        in_specs=[vmem()],
        out_specs=(vmem(), vmem()),
        compiler_params=params,
        name="lead_prep",
    )(jnp.concatenate([child_tiles[:, :, :edge], mask_tile], axis=0))

    if col_count == PANELS:
        lead_own = lead
        lead_other = lax.ppermute(lead, "col", [(i, 1 - i) for i in range(PANELS)])
    else:
        gathered = lax.all_gather(lead, "col")
        lead_own, lead_other = gathered[0], gathered[1]

    swap = col_count == PANELS
    gram_rows = edge * edge // width
    factor = pltpu.VMEM((4 * edge, rows), BF16)
    work = pl.CostEstimate(flops=12 * edge * rows * columns, bytes_accessed=4 * rows * columns, transcendentals=0)

    def sums(extra):
        return jax.ShapeDtypeStruct((pieces, edge + extra, width), F32)

    halves = jax.ShapeDtypeStruct((rows, columns), BF16)
    keep, send, high, low, mine = pl.pallas_call(
        functools.partial(own_kernel, row_count),
        out_shape=(sums(gram_rows), sums(gram_rows), halves, halves, jax.ShapeDtypeStruct((1, rows), F32)),
        in_specs=[smem(), smem(), vmem(), vmem(), pl.BlockSpec(memory_space=pl.ANY)],
        out_specs=(vmem(),) * 5,
        scratch_shapes=[
            factor,
            pltpu.VMEM((tile_count, edge, columns), F32),
            pltpu.VMEM((tile_count, columns), F32),
            pltpu.VMEM((2 * edge, columns), F32),
            pltpu.SemaphoreType.DMA((tile_count,)),
        ],
        compiler_params=wide_params,
        cost_estimate=work,
        name="panel_own",
    )(info, destination.reshape(1, tile_count), mask, lead_own, child_tiles)

    def over_leaf(keep, send):
        return keep + lax.ppermute(send, "leaf", [(0, 1), (1, 0)])

    def over_row(value, bit):
        return lax.ppermute(value, "row", [(i, i ^ bit) for i in range(row_count)])

    def reduce_near(partial, order):
        total = partial[0]
        for near in order:
            total = lax.optimization_barrier(total + over_row(partial[near], near))
        return total

    def reduce_far(total):
        for bit in range(split_bits, bits):
            total = total + over_row(total, 1 << bit | (mirror if bit == split_bits else 0))
        return total

    def gather_by_steps(total):
        held = [total[:edge]]
        for bit in range(1, split_bits):
            held = held + [over_row(piece, 1 << bit) for piece in held]
        return [piece for even in held for piece in (even, over_row(even, 1))]

    def gather_pieces(total):
        return [total[:edge]] + [over_row(total[:edge], near) for near in range(1, pieces)]

    send, lead_other = lax.optimization_barrier((send, lead_other))
    own_sum = reduce_far(reduce_near(over_leaf(keep, send), range(1, pieces)))
    own_pieces = gather_by_steps(own_sum)

    pair_rows = gram_rows if swap else 2 * gram_rows
    keep, send = pl.pallas_call(
        functools.partial(pair_kernel, not swap),
        out_shape=(sums(pair_rows), sums(pair_rows)),
        in_specs=[smem(), vmem(), vmem(), vmem(), vmem(), vmem()],
        out_specs=(vmem(),) * 2,
        scratch_shapes=[factor],
        compiler_params=params,
        cost_estimate=work,
        name="panel_pair",
    )(info, mine, lead_other, lead_own, high, low)
    other_sum = reduce_far(reduce_near(over_leaf(keep, send), range(1, pieces)))

    other_pieces = gather_pieces(other_sum)
    own_gram, pair_gram = own_sum[edge:], other_sum[edge:]
    if swap:
        other_gram, start = lax.ppermute(own_gram, "col", [(i, 1 - i) for i in range(PANELS)]), 0
    else:
        other_gram, start = pair_gram, edge // 16
    inverse = pl.pallas_call(
        functools.partial(factor_kernel, start),
        out_shape=jax.ShapeDtypeStruct((2 * edge, 2 * edge), F32),
        in_specs=[smem()] + [vmem()] * 3,
        out_specs=vmem(),
        compiler_params=params,
        name="gram_factor",
    )(info, own_gram, other_gram, pair_gram)

    return pl.pallas_call(
        functools.partial(final_kernel, pieces, edge),
        out_shape=jax.ShapeDtypeStruct((1, 2 * edge, columns), F32),
        in_specs=[smem(), vmem()] + [vmem()] * (2 * pieces),
        out_specs=pl.BlockSpec(memory_space=pl.ANY),
        scratch_shapes=[pltpu.VMEM((pieces, 2 * edge, width), F32), pltpu.SemaphoreType.DMA((pieces,))],
        compiler_params=params,
        name="apply_inverse",
    )(info, inverse, *own_pieces, *other_pieces)


def solution(mesh):
    in_specs = (
        P(("leaf", "row"), None, "col"),
        P(("leaf", "row"), "col"),
        P(("leaf", "row"), None),
    )
    out_specs = P("leaf", None, "col")
    return jax.shard_map(per_device, mesh=mesh, in_specs=in_specs, out_specs=out_specs, check_vma=False)
```

```python
import functools

import jax
import jax.numpy as jnp
from jax import lax
from jax.experimental import pallas as pl
from jax.experimental.pallas import tpu as pltpu
from jax.sharding import PartitionSpec as P

PANELS = 2
VMEM_LIMIT = 16 * 1024 * 1024
OWN_VMEM_LIMIT = 44 * 1024 * 1024
F32 = jnp.float32
BF16 = jnp.bfloat16
HIGHEST = lax.Precision.HIGHEST


def split(value):
    high = value.astype(BF16)
    return high, (value - high.astype(F32)).astype(BF16)


def dot_nt(a, b):
    return lax.dot_general(a, b, (((1,), (1,)), ((), ())), precision=HIGHEST, preferred_element_type=F32)


def prep_kernel(lead_ref, flipped_ref, mask_ref):
    edge = flipped_ref.shape[0]
    tile_count, blocks = mask_ref.shape
    mask = lead_ref[tile_count, :tile_count, :blocks]
    mask_ref[...] = mask
    flipped_ref[...] = (lead_ref[:tile_count] * mask[:, :1].reshape(tile_count, 1, 1)).reshape(-1, edge).T


def spread_mask(mask, columns, edge):
    blocks = mask.shape[1]
    over = lax.broadcasted_iota(jnp.int32, (blocks, columns), 1) // edge
    over = (over == lax.broadcasted_iota(jnp.int32, (blocks, columns), 0)).astype(F32)
    return jnp.dot(mask, over, preferred_element_type=F32)


def spread_front(dest_ref, leaf, per_front, rows):
    tile_count = dest_ref.shape[1]
    place = lax.broadcasted_iota(jnp.int32, (1, rows), 1) // (rows // tile_count)
    mine = jnp.zeros((1, rows), F32)
    for tile in range(tile_count):
        here = (dest_ref[0, tile] // per_front == leaf).astype(F32)
        mine = jnp.where(place == tile, here, mine)
    return mine


def by_front(lead, mine):
    return lead * mine, lead * (1.0 - mine)


def fill_factor(lhs, kept, sent, edge):
    for place, part in enumerate((kept, sent)):
        part_high, part_low = split(part)
        lhs[place * edge : (place + 1) * edge] = part_high
        lhs[(place + 2) * edge : (place + 3) * edge] = part_low


def panel_product(lhs, high, low, edge):
    big = jnp.dot(lhs, high, preferred_element_type=F32)
    small = jnp.dot(lhs[: 2 * edge], low, preferred_element_type=F32)
    return big[: 2 * edge] + (big[2 * edge :] + small)


def put_gram(blocks, out, edge):
    for near in range(out.shape[0]):
        place_slabs(blocks, out.at[near, edge:])


def halves_beside(block):
    return jnp.concatenate([block[: block.shape[0] // 2], block[block.shape[0] // 2 :]], axis=1)


def own_kernel(per_front, info_ref, dest_ref, mask_ref, lead_ref, tiles_ref, keep_ref, send_ref, high, low, mine_ref, lhs, held, wide_ref, total_ref, sems):
    tile_count, edge, columns = held.shape
    pieces, _, width = keep_ref.shape
    copies = [pltpu.make_async_copy(tiles_ref.at[tile], held.at[tile], sems.at[tile]) for tile in range(tile_count)]
    for copy in copies:
        copy.start()
    wide_ref[...] = spread_mask(mask_ref[...], columns, edge)
    mine_ref[...] = spread_front(dest_ref, info_ref[1], per_front, lead_ref.shape[1])
    lead = lead_ref[...]
    parts = by_front(lead, mine_ref[...])
    fill_factor(lhs, *parts, edge)
    gram = dot_nt(jnp.concatenate(parts, axis=0), lead)
    put_gram(halves_beside(gram[:edge]), keep_ref, edge)
    put_gram(halves_beside(gram[edge:]), send_ref, edge)
    cuts = (0, tile_count // 2, tile_count)
    for first, after in zip(cuts, cuts[1:]):
        for tile in range(first, after):
            copies[tile].wait()
            value = held[tile] * wide_ref[tile : tile + 1, :]
            value_high, value_low = split(value)
            high[tile * edge : (tile + 1) * edge] = value_high
            low[tile * edge : (tile + 1) * edge] = value_low
        deep = slice(first * edge, after * edge)
        for piece in range(pieces):
            here = slice(piece * width, (piece + 1) * width)
            part = panel_product(lhs[:, deep], high[deep, here], low[deep, here], edge)
            if after < tile_count:
                total_ref[:, here] = part if first == 0 else total_ref[:, here] + part
                continue
            total = total_ref[:, here] + part if first else part
            near = jnp.bitwise_xor(info_ref[0], piece)
            keep_ref[near, :edge] = total[:edge]
            send_ref[near, :edge] = total[edge:]


def pair_kernel(with_other, info_ref, mine_ref, lead_ref, own_ref, high, low, keep_ref, send_ref, lhs):
    edge = lead_ref.shape[0]
    pieces, _, width = keep_ref.shape
    lead, own = lead_ref[...], own_ref[...]
    parts = by_front(lead, mine_ref[...])
    fill_factor(lhs, *parts, edge)
    both = jnp.concatenate(parts, axis=0)
    cross = dot_nt(both, own)
    other = dot_nt(both, lead) if with_other else None
    for place, out in enumerate((keep_ref, send_ref)):
        here = slice(place * edge, (place + 1) * edge)
        blocks = halves_beside(cross[here])
        if with_other:
            blocks = jnp.concatenate([blocks, halves_beside(other[here])], axis=0)
        put_gram(blocks, out, edge)
    for piece in range(pieces):
        here = slice(piece * width, (piece + 1) * width)
        total = panel_product(lhs[...], high[:, here], low[:, here], edge)
        near = jnp.bitwise_xor(info_ref[0], piece)
        keep_ref[near, :edge] = total[:edge]
        send_ref[near, :edge] = total[edge:]


def place_slabs(value, out):
    across = out.shape[1] // value.shape[1]
    for slab in range(value.shape[0] // 8):
        down, right = slab // across, slab % across
        out[down * 8 : (down + 1) * 8, right * 128 : (right + 1) * 128] = value[slab * 8 : (slab + 1) * 8]


def take_block(ref, edge, start=0):
    across = ref.shape[1] // 128
    slabs = []
    for slab in range(start, start + edge // 16):
        down, right = slab // across, slab % across
        slabs.append(ref[down * 8 : (down + 1) * 8, right * 128 : (right + 1) * 128])
    value = jnp.concatenate(slabs, axis=0)
    return jnp.concatenate([value[:, :edge], value[:, edge:]], axis=0)


STEP = 8


def inverse_factor(whole, put):
    size = whole.shape[0]
    groups = size // 8
    rows = [whole[8 * i : 8 * i + 8] for i in range(groups)]
    lane = lax.broadcasted_iota(jnp.int32, (8, size), 1)
    down = lax.broadcasted_iota(jnp.int32, (8, size), 0)
    span = range(STEP)
    for k in range(0, size, STEP):
        group, inside = k // 8, k % 8
        pivot = [jnp.broadcast_to(rows[group][inside + j : inside + j + 1], (8, size)) for j in span]
        entry = [[jnp.broadcast_to(pivot[i][:, k + j : k + j + 1], (8, size)) for j in range(i + 1)] for i in span]
        ratio = [[None] * STEP for _ in span]
        inverse = [None] * STEP
        for j in span:
            inverse[j] = 1.0 / entry[j][j]
            for i in range(j + 1, STEP):
                ratio[i][j] = entry[i][j] * inverse[j]
            for i in range(j + 1, STEP):
                for m in range(j + 1, i + 1):
                    entry[i][m] = entry[i][m] - entry[i][j] * entry[m][j] * inverse[j]
        solved = []
        for j in span:
            unit = jnp.where(lane < k, pivot[j], jnp.where(lane == k + j, 1.0, 0.0))
            for i in range(j):
                unit = unit - ratio[j][i] * solved[i]
            solved.append(unit)
            put(k + j, (unit * lax.rsqrt(entry[j][j]))[:1])
        if k + STEP == size:
            break
        front = [jnp.where(lane == k + j, pivot[j] + 1.0, pivot[j]) for j in span]
        for j in span:
            for i in range(j):
                front[j] = front[j] - ratio[j][i] * front[i]
        back = [front[j] * inverse[j] for j in span]
        for j in reversed(span):
            for i in reversed(range(j + 1, STEP)):
                back[j] = back[j] - ratio[i][j] * back[i]
        for g in range((k + STEP) // 8, groups):
            row = rows[g]
            for j in reversed(span):
                row = row - jnp.broadcast_to(rows[g][:, k + j : k + j + 1], (8, size)) * back[j]
            rows[g] = jnp.where(down < inside + STEP, rows[g], row) if g == group else row


def both_grams(info_ref, own_ref, other_ref, other_start, edge):
    own, other = take_block(own_ref, edge), take_block(other_ref, edge, other_start)
    first = info_ref[2] == 0
    return jnp.where(first, own, other), jnp.where(first, other, own)


def factor_kernel(start, info_ref, own_ref, other_ref, pair_ref, out_ref):
    edge = out_ref.shape[0] // 2
    gram_00, gram_11 = both_grams(info_ref, own_ref, other_ref, start, edge)
    cross = take_block(pair_ref, edge)
    cross = jnp.where(info_ref[2] == 0, cross, cross.T)
    upper = jnp.concatenate([gram_00, cross.T], axis=1)
    lower = jnp.concatenate([cross, gram_11], axis=1)

    def put(index, row):
        out_ref[index : index + 1] = row

    inverse_factor(jnp.concatenate([upper, lower], axis=0), put)


def final_kernel(pieces, edge, info_ref, inverse_ref, *refs):
    own_refs, other_refs, (out_ref, held, sems) = refs[:pieces], refs[pieces : 2 * pieces], refs[2 * pieces :]
    width = own_refs[0].shape[1]
    inverse = inverse_ref[...]
    first = info_ref[2] == 0
    left, right = inverse[:, :edge], inverse[:, edge:]
    inverse = jnp.concatenate([jnp.where(first, left, right), jnp.where(first, right, left)], axis=1)
    inverse_high, inverse_low = split(inverse)
    both = jnp.concatenate([inverse_high, inverse_low], axis=0)
    row = lax.broadcasted_iota(jnp.int32, (2 * edge, width), 0)
    lane = lax.broadcasted_iota(jnp.int32, (2 * edge, width), 1)
    copies = []
    for near in range(pieces):
        part = jnp.concatenate([own_refs[near][:edge], other_refs[near][:edge]], axis=0)
        part_high, part_low = split(part)
        product = jnp.dot(both, part_high, preferred_element_type=F32)
        small = jnp.dot(inverse_high, part_low, preferred_element_type=F32)
        product = product[: 2 * edge] + (product[2 * edge :] + small)
        place = jnp.bitwise_xor(info_ref[0], near)
        place_lane = lane + place * width
        early = (place_lane < edge) & (place_lane + info_ref[3] * edge < row)
        held[near] = jnp.where(early, 0.0, product)
        copy = pltpu.make_async_copy(
            held.at[near],
            out_ref.at[0, :, pl.ds(pl.multiple_of(place * width, width), width)],
            sems.at[near],
        )
        copy.start()
        copies.append(copy)
    for copy in copies:
        copy.wait()


def vmem():
    return pl.BlockSpec(memory_space=pltpu.VMEM)


def smem():
    return pl.BlockSpec(memory_space=pltpu.SMEM)


def per_device(child_tiles, block_mask, destination):
    tile_count, edge, columns = child_tiles.shape
    rows = tile_count * edge
    row_count, col_count = lax.axis_size("row"), lax.axis_size("col")
    bits = row_count.bit_length() - 1
    split_bits = min(2, bits - 1, (columns // 128).bit_length() - 1)
    pieces = 1 << split_bits
    width = columns // pieces
    row, leaf, col = lax.axis_index("row"), lax.axis_index("leaf"), lax.axis_index("col")
    own_panel = col if col_count == PANELS else jnp.zeros_like(col)
    mirror = pieces // 2
    piece = row % pieces ^ (row // pieces % 2 * mirror)
    info = jnp.stack([piece, leaf, own_panel, col]).astype(jnp.int32)
    params = pltpu.CompilerParams(vmem_limit_bytes=VMEM_LIMIT)
    wide_params = pltpu.CompilerParams(vmem_limit_bytes=OWN_VMEM_LIMIT)

    blocks = columns // edge
    mask_tile = jnp.pad(block_mask.astype(F32), ((0, edge - tile_count), (0, edge - blocks)))[None]
    lead, mask = pl.pallas_call(
        prep_kernel,
        out_shape=(jax.ShapeDtypeStruct((edge, rows), F32), jax.ShapeDtypeStruct((tile_count, blocks), F32)),
        in_specs=[vmem()],
        out_specs=(vmem(), vmem()),
        compiler_params=params,
        name="lead_prep",
    )(jnp.concatenate([child_tiles[:, :, :edge], mask_tile], axis=0))

    if col_count == PANELS:
        lead_own = lead
        lead_other = lax.ppermute(lead, "col", [(i, 1 - i) for i in range(PANELS)])
    else:
        gathered = lax.all_gather(lead, "col")
        lead_own, lead_other = gathered[0], gathered[1]

    swap = col_count == PANELS
    gram_rows = edge * edge // width
    factor = pltpu.VMEM((4 * edge, rows), BF16)
    work = pl.CostEstimate(flops=12 * edge * rows * columns, bytes_accessed=4 * rows * columns, transcendentals=0)

    def sums(extra):
        return jax.ShapeDtypeStruct((pieces, edge + extra, width), F32)

    halves = jax.ShapeDtypeStruct((rows, columns), BF16)
    keep, send, high, low, mine = pl.pallas_call(
        functools.partial(own_kernel, row_count),
        out_shape=(sums(gram_rows), sums(gram_rows), halves, halves, jax.ShapeDtypeStruct((1, rows), F32)),
        in_specs=[smem(), smem(), vmem(), vmem(), pl.BlockSpec(memory_space=pl.ANY)],
        out_specs=(vmem(),) * 5,
        scratch_shapes=[
            factor,
            pltpu.VMEM((tile_count, edge, columns), F32),
            pltpu.VMEM((tile_count, columns), F32),
            pltpu.VMEM((2 * edge, columns), F32),
            pltpu.SemaphoreType.DMA((tile_count,)),
        ],
        compiler_params=wide_params,
        cost_estimate=work,
        name="panel_own",
    )(info, destination.reshape(1, tile_count), mask, lead_own, child_tiles)

    def over_leaf(keep, send):
        return keep + lax.ppermute(send, "leaf", [(0, 1), (1, 0)])

    def over_row(value, bit):
        return lax.ppermute(value, "row", [(i, i ^ bit) for i in range(row_count)])

    def reduce_near(partial, order):
        total = partial[0]
        for near in order:
            total = lax.optimization_barrier(total + over_row(partial[near], near))
        return total

    def reduce_far(total):
        for bit in range(split_bits, bits):
            total = total + over_row(total, 1 << bit | (mirror if bit == split_bits else 0))
        return total

    def gather_by_steps(total):
        held = [total[:edge]]
        for bit in range(1, split_bits):
            held = held + [over_row(piece, 1 << bit) for piece in held]
        return [piece for even in held for piece in (even, over_row(even, 1))]

    def gather_pieces(total):
        return [total[:edge]] + [over_row(total[:edge], near) for near in range(1, pieces)]

    send, lead_other = lax.optimization_barrier((send, lead_other))
    own_sum = reduce_far(reduce_near(over_leaf(keep, send), range(1, pieces)))
    own_pieces = gather_by_steps(own_sum)

    pair_rows = gram_rows if swap else 2 * gram_rows
    keep, send = pl.pallas_call(
        functools.partial(pair_kernel, not swap),
        out_shape=(sums(pair_rows), sums(pair_rows)),
        in_specs=[smem(), vmem(), vmem(), vmem(), vmem(), vmem()],
        out_specs=(vmem(),) * 2,
        scratch_shapes=[factor],
        compiler_params=params,
        cost_estimate=work,
        name="panel_pair",
    )(info, mine, lead_other, lead_own, high, low)
    other_sum = reduce_far(reduce_near(over_leaf(keep, send), range(1, pieces)))

    other_pieces = gather_pieces(other_sum)
    own_gram, pair_gram = own_sum[edge:], other_sum[edge:]
    if swap:
        other_gram, start = lax.ppermute(own_gram, "col", [(i, 1 - i) for i in range(PANELS)]), 0
    else:
        other_gram, start = pair_gram, edge // 16
    inverse = pl.pallas_call(
        functools.partial(factor_kernel, start),
        out_shape=jax.ShapeDtypeStruct((2 * edge, 2 * edge), F32),
        in_specs=[smem()] + [vmem()] * 3,
        out_specs=vmem(),
        compiler_params=params,
        name="gram_factor",
    )(info, own_gram, other_gram, pair_gram)

    return pl.pallas_call(
        functools.partial(final_kernel, pieces, edge),
        out_shape=jax.ShapeDtypeStruct((1, 2 * edge, columns), F32),
        in_specs=[smem(), vmem()] + [vmem()] * (2 * pieces),
        out_specs=pl.BlockSpec(memory_space=pl.ANY),
        scratch_shapes=[pltpu.VMEM((pieces, 2 * edge, width), F32), pltpu.SemaphoreType.DMA((pieces,))],
        compiler_params=params,
        name="apply_inverse",
    )(info, inverse, *own_pieces, *other_pieces)


def solution(mesh):
    in_specs = (
        P(("leaf", "row"), None, "col"),
        P(("leaf", "row"), "col"),
        P(("leaf", "row"), None),
    )
    out_specs = P("leaf", None, "col")
    return jax.shard_map(per_device, mesh=mesh, in_specs=in_specs, out_specs=out_specs, check_vma=False)
```

```python
import functools

import jax
import jax.numpy as jnp
from jax import lax
from jax.experimental import pallas as pl
from jax.experimental.pallas import tpu as pltpu
from jax.sharding import PartitionSpec as P

PANELS = 2
VMEM_LIMIT = 16 * 1024 * 1024
OWN_VMEM_LIMIT = 44 * 1024 * 1024
F32 = jnp.float32
BF16 = jnp.bfloat16
HIGHEST = lax.Precision.HIGHEST


def split(value):
    high = value.astype(BF16)
    return high, (value - high.astype(F32)).astype(BF16)


def dot_nt(a, b):
    return lax.dot_general(a, b, (((1,), (1,)), ((), ())), precision=HIGHEST, preferred_element_type=F32)


def prep_kernel(lead_ref, flipped_ref, mask_ref):
    edge = flipped_ref.shape[0]
    tile_count, blocks = mask_ref.shape
    mask = lead_ref[tile_count, :tile_count, :blocks]
    mask_ref[...] = mask
    flipped_ref[...] = (lead_ref[:tile_count] * mask[:, :1].reshape(tile_count, 1, 1)).reshape(-1, edge).T


def spread_mask(mask, columns, edge):
    blocks = mask.shape[1]
    over = lax.broadcasted_iota(jnp.int32, (blocks, columns), 1) // edge
    over = (over == lax.broadcasted_iota(jnp.int32, (blocks, columns), 0)).astype(F32)
    return jnp.dot(mask, over, preferred_element_type=F32)


def spread_front(dest_ref, leaf, per_front, rows):
    tile_count = dest_ref.shape[1]
    place = lax.broadcasted_iota(jnp.int32, (1, rows), 1) // (rows // tile_count)
    mine = jnp.zeros((1, rows), F32)
    for tile in range(tile_count):
        here = (dest_ref[0, tile] // per_front == leaf).astype(F32)
        mine = jnp.where(place == tile, here, mine)
    return mine


def by_front(lead, mine):
    return lead * mine, lead * (1.0 - mine)


def fill_factor(lhs, kept, sent, edge):
    for place, part in enumerate((kept, sent)):
        part_high, part_low = split(part)
        lhs[place * edge : (place + 1) * edge] = part_high
        lhs[(place + 2) * edge : (place + 3) * edge] = part_low


def panel_product(lhs, high, low, edge):
    big = jnp.dot(lhs, high, preferred_element_type=F32)
    small = jnp.dot(lhs[: 2 * edge], low, preferred_element_type=F32)
    return big[: 2 * edge] + (big[2 * edge :] + small)


def put_gram(blocks, out, edge):
    for near in range(out.shape[0]):
        place_slabs(blocks, out.at[near, edge:])


def halves_beside(block):
    return jnp.concatenate([block[: block.shape[0] // 2], block[block.shape[0] // 2 :]], axis=1)


def own_kernel(per_front, info_ref, dest_ref, mask_ref, lead_ref, tiles_ref, keep_ref, send_ref, high, low, mine_ref, lhs, held, wide_ref, total_ref, sems):
    tile_count, edge, columns = held.shape
    pieces, _, width = keep_ref.shape
    copies = [pltpu.make_async_copy(tiles_ref.at[tile], held.at[tile], sems.at[tile]) for tile in range(tile_count)]
    for copy in copies:
        copy.start()
    wide_ref[...] = spread_mask(mask_ref[...], columns, edge)
    mine_ref[...] = spread_front(dest_ref, info_ref[1], per_front, lead_ref.shape[1])
    lead = lead_ref[...]
    parts = by_front(lead, mine_ref[...])
    fill_factor(lhs, *parts, edge)
    gram = dot_nt(jnp.concatenate(parts, axis=0), lead)
    put_gram(halves_beside(gram[:edge]), keep_ref, edge)
    put_gram(halves_beside(gram[edge:]), send_ref, edge)
    cuts = (0, tile_count // 2, tile_count)
    for first, after in zip(cuts, cuts[1:]):
        for tile in range(first, after):
            copies[tile].wait()
            value = held[tile] * wide_ref[tile : tile + 1, :]
            value_high, value_low = split(value)
            high[tile * edge : (tile + 1) * edge] = value_high
            low[tile * edge : (tile + 1) * edge] = value_low
        deep = slice(first * edge, after * edge)
        for piece in range(pieces):
            here = slice(piece * width, (piece + 1) * width)
            part = panel_product(lhs[:, deep], high[deep, here], low[deep, here], edge)
            if after < tile_count:
                total_ref[:, here] = part if first == 0 else total_ref[:, here] + part
                continue
            total = total_ref[:, here] + part if first else part
            near = jnp.bitwise_xor(info_ref[0], piece)
            keep_ref[near, :edge] = total[:edge]
            send_ref[near, :edge] = total[edge:]


def pair_kernel(with_other, info_ref, mine_ref, lead_ref, own_ref, high, low, keep_ref, send_ref, lhs):
    edge = lead_ref.shape[0]
    pieces, _, width = keep_ref.shape
    lead, own = lead_ref[...], own_ref[...]
    parts = by_front(lead, mine_ref[...])
    fill_factor(lhs, *parts, edge)
    both = jnp.concatenate(parts, axis=0)
    cross = dot_nt(both, own)
    other = dot_nt(both, lead) if with_other else None
    for place, out in enumerate((keep_ref, send_ref)):
        here = slice(place * edge, (place + 1) * edge)
        blocks = halves_beside(cross[here])
        if with_other:
            blocks = jnp.concatenate([blocks, halves_beside(other[here])], axis=0)
        put_gram(blocks, out, edge)
    for piece in range(pieces):
        here = slice(piece * width, (piece + 1) * width)
        total = panel_product(lhs[...], high[:, here], low[:, here], edge)
        near = jnp.bitwise_xor(info_ref[0], piece)
        keep_ref[near, :edge] = total[:edge]
        send_ref[near, :edge] = total[edge:]


def place_slabs(value, out):
    across = out.shape[1] // value.shape[1]
    for slab in range(value.shape[0] // 8):
        down, right = slab // across, slab % across
        out[down * 8 : (down + 1) * 8, right * 128 : (right + 1) * 128] = value[slab * 8 : (slab + 1) * 8]


def take_block(ref, edge, start=0):
    across = ref.shape[1] // 128
    slabs = []
    for slab in range(start, start + edge // 16):
        down, right = slab // across, slab % across
        slabs.append(ref[down * 8 : (down + 1) * 8, right * 128 : (right + 1) * 128])
    value = jnp.concatenate(slabs, axis=0)
    return jnp.concatenate([value[:, :edge], value[:, edge:]], axis=0)


STEP = 8


def inverse_factor(whole, put):
    size = whole.shape[0]
    groups = size // 8
    rows = [whole[8 * i : 8 * i + 8] for i in range(groups)]
    lane = lax.broadcasted_iota(jnp.int32, (8, size), 1)
    down = lax.broadcasted_iota(jnp.int32, (8, size), 0)
    span = range(STEP)
    for k in range(0, size, STEP):
        group, inside = k // 8, k % 8
        pivot = [jnp.broadcast_to(rows[group][inside + j : inside + j + 1], (8, size)) for j in span]
        entry = [[jnp.broadcast_to(pivot[i][:, k + j : k + j + 1], (8, size)) for j in range(i + 1)] for i in span]
        ratio = [[None] * STEP for _ in span]
        inverse = [None] * STEP
        for j in span:
            inverse[j] = 1.0 / entry[j][j]
            for i in range(j + 1, STEP):
                ratio[i][j] = entry[i][j] * inverse[j]
            for i in range(j + 1, STEP):
                for m in range(j + 1, i + 1):
                    entry[i][m] = entry[i][m] - entry[i][j] * entry[m][j] * inverse[j]
        solved = []
        for j in span:
            unit = jnp.where(lane < k, pivot[j], jnp.where(lane == k + j, 1.0, 0.0))
            for i in range(j):
                unit = unit - ratio[j][i] * solved[i]
            solved.append(unit)
            put(k + j, (unit * lax.rsqrt(entry[j][j]))[:1])
        if k + STEP == size:
            break
        front = [jnp.where(lane == k + j, pivot[j] + 1.0, pivot[j]) for j in span]
        for j in span:
            for i in range(j):
                front[j] = front[j] - ratio[j][i] * front[i]
        back = [front[j] * inverse[j] for j in span]
        for j in reversed(span):
            for i in reversed(range(j + 1, STEP)):
                back[j] = back[j] - ratio[i][j] * back[i]
        for g in range((k + STEP) // 8, groups):
            row = rows[g]
            for j in reversed(span):
                row = row - jnp.broadcast_to(rows[g][:, k + j : k + j + 1], (8, size)) * back[j]
            rows[g] = jnp.where(down < inside + STEP, rows[g], row) if g == group else row


def both_grams(info_ref, own_ref, other_ref, other_start, edge):
    own, other = take_block(own_ref, edge), take_block(other_ref, edge, other_start)
    first = info_ref[2] == 0
    return jnp.where(first, own, other), jnp.where(first, other, own)


def factor_kernel(start, info_ref, own_ref, other_ref, pair_ref, out_ref):
    edge = out_ref.shape[0] // 2
    gram_00, gram_11 = both_grams(info_ref, own_ref, other_ref, start, edge)
    cross = take_block(pair_ref, edge)
    cross = jnp.where(info_ref[2] == 0, cross, cross.T)
    upper = jnp.concatenate([gram_00, cross.T], axis=1)
    lower = jnp.concatenate([cross, gram_11], axis=1)

    def put(index, row):
        out_ref[index : index + 1] = row

    inverse_factor(jnp.concatenate([upper, lower], axis=0), put)


def final_kernel(pieces, edge, info_ref, inverse_ref, *refs):
    own_refs, other_refs, (out_ref, held, sems) = refs[:pieces], refs[pieces : 2 * pieces], refs[2 * pieces :]
    width = own_refs[0].shape[1]
    inverse = inverse_ref[...]
    first = info_ref[2] == 0
    left, right = inverse[:, :edge], inverse[:, edge:]
    inverse = jnp.concatenate([jnp.where(first, left, right), jnp.where(first, right, left)], axis=1)
    inverse_high, inverse_low = split(inverse)
    three = jnp.concatenate([inverse_high, inverse_high, inverse_low], axis=1)
    row = lax.broadcasted_iota(jnp.int32, (2 * edge, width), 0)
    lane = lax.broadcasted_iota(jnp.int32, (2 * edge, width), 1)
    copies = []
    for near in range(pieces):
        part = jnp.concatenate([own_refs[near][:edge], other_refs[near][:edge]], axis=0)
        part_high, part_low = split(part)
        stacked = jnp.concatenate([part_high, part_low, part_high], axis=0)
        product = jnp.dot(three, stacked, preferred_element_type=F32)
        place = jnp.bitwise_xor(info_ref[0], near)
        place_lane = lane + place * width
        early = (place_lane < edge) & (place_lane + info_ref[3] * edge < row)
        held[near] = jnp.where(early, 0.0, product)
        copy = pltpu.make_async_copy(
            held.at[near],
            out_ref.at[0, :, pl.ds(pl.multiple_of(place * width, width), width)],
            sems.at[near],
        )
        copy.start()
        copies.append(copy)
    for copy in copies:
        copy.wait()


def vmem():
    return pl.BlockSpec(memory_space=pltpu.VMEM)


def smem():
    return pl.BlockSpec(memory_space=pltpu.SMEM)


def per_device(child_tiles, block_mask, destination):
    tile_count, edge, columns = child_tiles.shape
    rows = tile_count * edge
    row_count, col_count = lax.axis_size("row"), lax.axis_size("col")
    bits = row_count.bit_length() - 1
    split_bits = min(2, bits - 1, (columns // 128).bit_length() - 1)
    pieces = 1 << split_bits
    width = columns // pieces
    row, leaf, col = lax.axis_index("row"), lax.axis_index("leaf"), lax.axis_index("col")
    own_panel = col if col_count == PANELS else jnp.zeros_like(col)
    mirror = pieces // 2
    piece = row % pieces ^ (row // pieces % 2 * mirror)
    info = jnp.stack([piece, leaf, own_panel, col]).astype(jnp.int32)
    params = pltpu.CompilerParams(vmem_limit_bytes=VMEM_LIMIT)
    wide_params = pltpu.CompilerParams(vmem_limit_bytes=OWN_VMEM_LIMIT)

    blocks = columns // edge
    mask_tile = jnp.pad(block_mask.astype(F32), ((0, edge - tile_count), (0, edge - blocks)))[None]
    lead, mask = pl.pallas_call(
        prep_kernel,
        out_shape=(jax.ShapeDtypeStruct((edge, rows), F32), jax.ShapeDtypeStruct((tile_count, blocks), F32)),
        in_specs=[vmem()],
        out_specs=(vmem(), vmem()),
        compiler_params=params,
        name="lead_prep",
    )(jnp.concatenate([child_tiles[:, :, :edge], mask_tile], axis=0))

    if col_count == PANELS:
        lead_own = lead
        lead_other = lax.ppermute(lead, "col", [(i, 1 - i) for i in range(PANELS)])
    else:
        gathered = lax.all_gather(lead, "col")
        lead_own, lead_other = gathered[0], gathered[1]

    swap = col_count == PANELS
    gram_rows = edge * edge // width
    factor = pltpu.VMEM((4 * edge, rows), BF16)
    work = pl.CostEstimate(flops=12 * edge * rows * columns, bytes_accessed=4 * rows * columns, transcendentals=0)

    def sums(extra):
        return jax.ShapeDtypeStruct((pieces, edge + extra, width), F32)

    halves = jax.ShapeDtypeStruct((rows, columns), BF16)
    keep, send, high, low, mine = pl.pallas_call(
        functools.partial(own_kernel, row_count),
        out_shape=(sums(gram_rows), sums(gram_rows), halves, halves, jax.ShapeDtypeStruct((1, rows), F32)),
        in_specs=[smem(), smem(), vmem(), vmem(), pl.BlockSpec(memory_space=pl.ANY)],
        out_specs=(vmem(),) * 5,
        scratch_shapes=[
            factor,
            pltpu.VMEM((tile_count, edge, columns), F32),
            pltpu.VMEM((tile_count, columns), F32),
            pltpu.VMEM((2 * edge, columns), F32),
            pltpu.SemaphoreType.DMA((tile_count,)),
        ],
        compiler_params=wide_params,
        cost_estimate=work,
        name="panel_own",
    )(info, destination.reshape(1, tile_count), mask, lead_own, child_tiles)

    def over_leaf(keep, send):
        return keep + lax.ppermute(send, "leaf", [(0, 1), (1, 0)])

    def over_row(value, bit):
        return lax.ppermute(value, "row", [(i, i ^ bit) for i in range(row_count)])

    def reduce_near(partial, order):
        total = partial[0]
        for near in order:
            total = lax.optimization_barrier(total + over_row(partial[near], near))
        return total

    def reduce_far(total):
        for bit in range(split_bits, bits):
            total = total + over_row(total, 1 << bit | (mirror if bit == split_bits else 0))
        return total

    def gather_by_steps(total):
        held = [total[:edge]]
        for bit in range(1, split_bits):
            held = held + [over_row(piece, 1 << bit) for piece in held]
        return [piece for even in held for piece in (even, over_row(even, 1))]

    def gather_pieces(total):
        return [total[:edge]] + [over_row(total[:edge], near) for near in range(1, pieces)]

    send, lead_other = lax.optimization_barrier((send, lead_other))
    own_sum = reduce_far(reduce_near(over_leaf(keep, send), range(1, pieces)))
    own_pieces = gather_by_steps(own_sum)

    pair_rows = gram_rows if swap else 2 * gram_rows
    keep, send = pl.pallas_call(
        functools.partial(pair_kernel, not swap),
        out_shape=(sums(pair_rows), sums(pair_rows)),
        in_specs=[smem(), vmem(), vmem(), vmem(), vmem(), vmem()],
        out_specs=(vmem(),) * 2,
        scratch_shapes=[factor],
        compiler_params=params,
        cost_estimate=work,
        name="panel_pair",
    )(info, mine, lead_other, lead_own, high, low)
    other_sum = reduce_far(reduce_near(over_leaf(keep, send), range(1, pieces)))

    other_pieces = gather_pieces(other_sum)
    own_gram, pair_gram = own_sum[edge:], other_sum[edge:]
    if swap:
        other_gram, start = lax.ppermute(own_gram, "col", [(i, 1 - i) for i in range(PANELS)]), 0
    else:
        other_gram, start = pair_gram, edge // 16
    inverse = pl.pallas_call(
        functools.partial(factor_kernel, start),
        out_shape=jax.ShapeDtypeStruct((2 * edge, 2 * edge), F32),
        in_specs=[smem()] + [vmem()] * 3,
        out_specs=vmem(),
        compiler_params=params,
        name="gram_factor",
    )(info, own_gram, other_gram, pair_gram)

    return pl.pallas_call(
        functools.partial(final_kernel, pieces, edge),
        out_shape=jax.ShapeDtypeStruct((1, 2 * edge, columns), F32),
        in_specs=[smem(), vmem()] + [vmem()] * (2 * pieces),
        out_specs=pl.BlockSpec(memory_space=pl.ANY),
        scratch_shapes=[pltpu.VMEM((pieces, 2 * edge, width), F32), pltpu.SemaphoreType.DMA((pieces,))],
        compiler_params=params,
        name="apply_inverse",
    )(info, inverse, *own_pieces, *other_pieces)


def solution(mesh):
    in_specs = (
        P(("leaf", "row"), None, "col"),
        P(("leaf", "row"), "col"),
        P(("leaf", "row"), None),
    )
    out_specs = P("leaf", None, "col")
    return jax.shard_map(per_device, mesh=mesh, in_specs=in_specs, out_specs=out_specs, check_vma=False)
```
